512 devices in a mesh: space: 64 (over y, z_lo, core), sample: 8 (over z_hi, x).
Axes of the slice: x: 4, y: 8, z: 8 (z_hi: 2, z_lo: 4; z = z_hi * 4 + z_lo), core: 2. Of those that a mesh axis runs over, the one named last changes fastest.
Arguments:
- volume: bfloat16 [8, 64, 32, 2048], P('sample', 'space'), may hold values from -6 to 6
- weight: bfloat16 [3, 3, 3, 64, 128], replicated, may hold values from -0.15625 to 0.15625
- conv_bias: float32 [128], replicated, may hold values from -3 to 3
- cotangent: bfloat16 [8, 512, 16, 128], P('sample', 'space'), may hold values from -6 to 6
Outputs:
- pooled: bfloat16 [8, 512, 16, 128], P('sample', 'space')
- input_grad: bfloat16 [8, 64, 32, 2048], P('sample', 'space')
- weight_grad: float32 [3, 3, 3, 64, 128], replicated
- bias_grad: float32 [128], replicated
The draws below stay inside these ranges and needn't reach their ends.
All inputs are finite; a program needn't handle non-finite values.
Results may differ from the reference program's by a relative error of at most 0.013.
Values may be sent and summed in bfloat16 or wider, within the bound.
A program may use at most 64 MiB of HBM per device.

```python
import jax
import jax.numpy as jnp
from jax import lax

CIN = 64
COUT = 128
SIDE = 32
DEPTH = 64
SAMPLES = 8
HALF = 16


def steps_of(own_key, dims, split, least, top_value):
    def one(axis_at, shards_of):
        steps = jax.random.uniform(jax.random.fold_in(jax.random.fold_in(own_key, 6), axis_at), (shards_of,), jnp.float32, least / len(split), top_value / len(split))
        return jnp.repeat(jnp.exp(steps), dims[axis_at] // shards_of).reshape((-1,) + (1,) * (len(dims) - axis_at - 1))

    level = one(*split[0])
    for cut in split[1:]:
        level = level * one(*cut)
    return level


def bell_draw(own_key, shape, scale, limit, shards=(), kind=jnp.bfloat16):
    gain = steps_of(own_key, shape, shards, -0.22, 0.18) if shards else 1.0
    array = jax.random.normal(own_key, shape, jnp.float32) * scale * gain
    return jnp.minimum(jnp.maximum(array, -limit), limit).astype(kind)


def setup_inputs(seed: int = 0) -> dict:
    splits = jax.random.split(jax.random.key(seed), 5)
    volume = bell_draw(splits[0], (SAMPLES, DEPTH, SIDE, SIDE * CIN), 1.0, 6.0, ((0, 8), (1, 64)))
    weight = bell_draw(splits[1], (3, 3, 3, CIN, COUT), (27 * CIN) ** -0.5, 0.15625)
    conv_bias = bell_draw(splits[2], (COUT,), 0.5, 3.0, (), jnp.float32)
    cotangent = bell_draw(splits[3], (SAMPLES, DEPTH // 2 * HALF, HALF, COUT), 1.0, 6.0, ((0, 8), (1, 64)))
    return dict(volume=volume, weight=weight, conv_bias=conv_bias, cotangent=cotangent)


loss_scale = 256.0


def conv_volume(volume_cells, weight):
    result = lax.conv_general_dilated(volume_cells[None], weight, (1, 1, 1), ((1, 1), (1, 1), (1, 1)), dimension_numbers=("NDHWC", "DHWIO", "NDHWC"), preferred_element_type=jnp.float32)
    return result[0]


def back_taps(grad_pre, weight_tap):
    flipped = jnp.transpose(weight_tap[::-1, ::-1], (0, 1, 3, 2))
    result = lax.conv_general_dilated(grad_pre, flipped, (1, 1), ((1, 1), (1, 1)), dimension_numbers=("NHWC", "HWIO", "NHWC"), preferred_element_type=jnp.float32)
    return lax.optimization_barrier(result.astype(jnp.bfloat16))


def one_sample(weight, conv_bias, sample_items):
    volume, cotangent = sample_items
    volume_cells = volume.reshape(DEPTH, SIDE, SIDE, CIN)
    pre_act = conv_volume(volume_cells, weight) + conv_bias
    sigmoid_pre = jax.nn.sigmoid(pre_act)
    activation = pre_act * sigmoid_pre
    windows = activation.reshape(DEPTH // 2, 2, HALF, 2, HALF, 2, COUT)
    exp_act = jnp.exp(windows)
    numerator = jnp.sum(exp_act * windows, axis=(1, 3, 5))
    denominator = jnp.sum(exp_act, axis=(1, 3, 5))
    pool_value = numerator / denominator
    pooled = pool_value.astype(jnp.bfloat16).reshape(DEPTH // 2 * HALF, HALF, COUT)
    upstream = cotangent.astype(jnp.float32).reshape(DEPTH // 2, HALF, HALF, COUT)
    coef_b = upstream / denominator
    coef_a = coef_b * (1.0 - pool_value)
    spread_a = coef_a[:, None, :, None, :, None, :]
    spread_b = coef_b[:, None, :, None, :, None, :]
    grad_act = (exp_act * (spread_a + spread_b * windows)).reshape(DEPTH, SIDE, SIDE, COUT)
    grad_pre = (grad_act * sigmoid_pre * (1.0 + pre_act * (1.0 - sigmoid_pre))).astype(jnp.bfloat16)
    grad_pre = lax.optimization_barrier(grad_pre)
    bias_part = jnp.sum(grad_pre.astype(jnp.float32), axis=(0, 1, 2))
    padded = jnp.pad(volume_cells, ((1, 1), (1, 1), (1, 1), (0, 0)))
    flat_grad = grad_pre.reshape(-1, COUT)
    tap_list = []
    for depth_tap in range(3):
        for row_tap in range(3):
            for col_tap in range(3):
                window = padded[depth_tap:depth_tap + DEPTH, row_tap:row_tap + SIDE, col_tap:col_tap + SIDE].reshape(-1, CIN)
                tap_list.append(jnp.dot(window.T, flat_grad, preferred_element_type=jnp.float32))
    weight_part = jnp.stack(tap_list).reshape(3, 3, 3, CIN, COUT)
    zero_plane = jnp.zeros((1, SIDE, SIDE, CIN), jnp.bfloat16)
    term_upper = back_taps(grad_pre, weight[0])
    term_middle = back_taps(grad_pre, weight[1])
    term_lower = back_taps(grad_pre, weight[2])
    from_above = jnp.concatenate([term_upper[1:], zero_plane], axis=0)
    from_below = jnp.concatenate([zero_plane, term_lower[:-1]], axis=0)
    summed = from_above.astype(jnp.float32) + term_middle.astype(jnp.float32) + from_below.astype(jnp.float32)
    input_grad = summed.astype(jnp.bfloat16).reshape(DEPTH, SIDE, SIDE * CIN)
    return pooled, input_grad, weight_part, bias_part


def reference(volume, weight, conv_bias, cotangent):
    def per_sample(sample_items):
        return one_sample(weight, conv_bias, sample_items)

    pooled, input_grad, weight_parts, bias_parts = lax.map(per_sample, (volume, cotangent))
    weight_grad = jnp.sum(weight_parts, axis=0) / loss_scale
    bias_grad = jnp.sum(bias_parts, axis=0) / loss_scale
    return pooled, input_grad, weight_grad, bias_grad
```

```python
import jax
import jax.numpy as jnp
from jax import lax
from jax.experimental import pallas as pl
from jax.experimental.pallas import tpu as pltpu
from jax.sharding import PartitionSpec as P

MESH = pl.DeviceIdType.MESH
BF16 = jnp.bfloat16
F32 = jnp.float32
taps = 27
pieces = 28
per_kind = 14
ring_order = (4, 3, 5, 2, 6, 1, 7)
plane_order = sorted(
    [(dx, dr) for dx in range(4) for dr in range(8) if (dx, dr) != (0, 0)],
    key=lambda d: -(min(d[0], 4 - d[0]) + min(d[1], 8 - d[1])),
)


def place():
    space = lax.axis_index("space")
    sample = lax.axis_index("sample")
    core = lax.rem(space, 2)
    z_lo = lax.rem(lax.div(space, 2), 4)
    y = lax.div(space, 8)
    z = lax.div(sample, 4) * 4 + z_lo
    x = lax.rem(sample, 4)
    return x, y, z, core


def ident(x, y, z, core):
    return ((y * 4 + lax.rem(z, 4)) * 2 + core, lax.div(z, 4) * 4 + x)


class Reduce:
    def __init__(self):
        self.x, self.y, self.z, self.core = place()
        x, y, z = self.x, self.y, self.z
        self.kind_a = x < 2
        self.ring_at = jnp.where(self.kind_a, z, y)
        self.row_at = jnp.where(self.kind_a, y, z)
        spot = lax.rem(x, 2) * 8 + self.row_at
        self.owner = spot < per_kind
        self.kind = jnp.where(self.kind_a, 0, 1)
        self.piece = jnp.minimum(self.kind * per_kind + spot, pieces - 1)
        self.slot = x * 8 + self.row_at
        self.partner = ident(x, y, z, 1 - self.core)

    def plane_peer(self, dx, dr):
        row = lax.rem(self.row_at + dr, 8)
        y = jnp.where(self.kind_a, row, self.y)
        z = jnp.where(self.kind_a, self.z, row)
        return ident(lax.rem(self.x + dx, 4), y, z, self.core)

    def ring_peer(self, dr):
        at = lax.rem(self.ring_at + dr, 8)
        y = jnp.where(self.kind_a, self.y, at)
        z = jnp.where(self.kind_a, at, self.z)
        return ident(self.x, y, z, self.core)

    def owner_of(self, piece):
        kind, spot = divmod(piece, per_kind)
        x = 2 * kind + spot // 8
        row = spot % 8
        if kind == 0:
            return ident(x, row, self.z, self.core), self.x * 8 + self.y
        return ident(x, self.y, row, self.core), self.x * 8 + self.z


def signal(sem, who):
    pl.semaphore_signal(sem, inc=1, device_id=who, device_id_type=MESH)


def remote(src, dst, send, recv, who):
    return pltpu.make_async_remote_copy(
        src_ref=src, dst_ref=dst, send_sem=send, recv_sem=recv, device_id=who, device_id_type=MESH
    )


def reduce_kernel(
    part_ref, total_ref, mine, theirs, rows, rs, ring_src, ring, final, gath,
    core_send, core_recv, rs_send, rs_recv, ring_send, ring_recv, ag_send, ag_recv, fw_send, fw_recv,
):
    r = Reduce()
    bar = pltpu.get_barrier_semaphore()

    @pl.when(r.owner)
    def _():
        for dx, dr in plane_order:
            signal(bar, r.plane_peer(dx, dr))
        for dr in ring_order:
            signal(bar, r.ring_peer(dr))

    signal(bar, r.partner)
    own = jnp.where(r.owner, 1, 0)
    pl.semaphore_wait(bar, pieces + 1 + 6 * own)

    half = r.core * 32
    far_half = 32 - half
    core_copies = []
    for g in range(4):
        span = pl.ds(7 * g, 7)
        mine[span] = part_ref[span, pl.ds(pl.multiple_of(far_half, 32), 32), :].astype(BF16)
        cp = remote(mine.at[span], theirs.at[span], core_send.at[g], core_recv.at[g], r.partner)
        cp.start()
        core_copies.append(cp)
    rs_copies = []
    for g in range(4):
        span = pl.ds(7 * g, 7)
        core_copies[g].wait_recv()
        rows[span] = (
            part_ref[span, pl.ds(pl.multiple_of(half, 32), 32), :] + theirs[span].astype(F32)
        ).astype(BF16)
        for piece in range(7 * g, 7 * g + 7):
            who, slot = r.owner_of(piece)
            is_me = jnp.logical_and(r.owner, r.piece == piece)
            cp = remote(rows.at[piece], rs.at[slot], rs_send.at[piece], rs_recv, who)
            rs_copies.append((is_me, cp))

            @pl.when(jnp.logical_not(is_me))
            def _(cp=cp):
                cp.start()

            @pl.when(is_me)
            def _(piece=piece):
                pltpu.make_async_copy(rows.at[piece], rs.at[r.slot], rs_recv).start()

    @pl.when(r.owner)
    def _():
        pltpu.make_async_copy(rs, rs, rs_recv).wait()
        total = rs[0].astype(F32)
        for i in range(1, 32):
            total = total + rs[i].astype(F32)
        ring_src[...] = total.astype(BF16)
        copies = []
        for dr in ring_order:
            cp = remote(ring_src, ring.at[r.ring_at], ring_send.at[dr], ring_recv, r.ring_peer(dr))
            cp.start()
            copies.append(cp)
        pltpu.make_async_copy(ring_src, ring.at[r.ring_at], ring_recv).start()
        pltpu.make_async_copy(ring, ring, ring_recv).wait()
        total = ring[0].astype(F32)
        for i in range(1, 8):
            total = total + ring[i].astype(F32)
        final[...] = total.astype(BF16)
        for i, (dx, dr) in enumerate(plane_order):
            cp = remote(
                final, gath.at[r.core, r.piece], ag_send.at[i], ag_recv.at[r.kind], r.plane_peer(dx, dr)
            )
            cp.start()
            copies.append(cp)
        pltpu.make_async_copy(final, gath.at[r.core, r.piece], ag_recv.at[r.kind]).start()
        for cp in copies:
            cp.wait_send()

    fw_copies = []
    for kind in range(2):
        span = gath.at[r.core, pl.ds(per_kind * kind, per_kind)]
        pltpu.make_async_copy(span, span, ag_recv.at[kind]).wait()
        cp = remote(span, span, fw_send.at[kind], fw_recv.at[kind], r.partner)
        cp.start()
        fw_copies.append(cp)
    for cp in core_copies:
        cp.wait_send()
    for is_me, cp in rs_copies:

        @pl.when(jnp.logical_not(is_me))
        def _(cp=cp):
            cp.wait_send()

    for cp in fw_copies:
        cp.wait()
    scale = 1.0 / loss_scale
    for h in range(2):
        total_ref[:, 32 * h : 32 * h + 32, :] = gath[h].astype(F32) * scale


def reduced(part):
    dma = pltpu.SemaphoreType.DMA
    return pl.pallas_call(
        reduce_kernel,
        out_shape=jax.ShapeDtypeStruct((pieces, 64, 128), F32),
        in_specs=[pl.BlockSpec(memory_space=pltpu.VMEM)],
        out_specs=pl.BlockSpec(memory_space=pltpu.VMEM),
        scratch_shapes=[
            pltpu.VMEM((pieces, 32, 128), BF16),
            pltpu.VMEM((pieces, 32, 128), BF16),
            pltpu.VMEM((pieces, 32, 128), BF16),
            pltpu.VMEM((32, 32, 128), BF16),
            pltpu.VMEM((32, 128), BF16),
            pltpu.VMEM((8, 32, 128), BF16),
            pltpu.VMEM((32, 128), BF16),
            pltpu.VMEM((2, pieces, 32, 128), BF16),
            dma((4,)), dma((4,)), dma((pieces,)), dma, dma((8,)), dma, dma((31,)), dma((2,)), dma((2,)), dma((2,)),
        ],
        compiler_params=pltpu.CompilerParams(
            collective_id=0, has_side_effects=True, vmem_limit_bytes=32 * 2**20
        ),
        name="reduce_weight_grad",
    )(part)


loss_scale = 256.0


def extended(value, sides, width):
    for axis, dim in sides:
        size, length = (lax.axis_size(axis), value.shape[dim])
        up = [(i, (i + 1) % size) for i in range(size - 1)]
        down = [(j, i) for i, j in up]
        last = lax.slice_in_dim(value, length - width, length, axis=dim)
        first = lax.slice_in_dim(value, 0, width, axis=dim)
        before = lax.ppermute(last, axis, up)
        after = lax.ppermute(first, axis, down)
        value = jnp.concatenate([before, value, after], axis=dim)
    return value


def partner(value, axis, bit):
    mask = 2**bit
    pairs = [(source, source ^ mask) for source in range(lax.axis_size(axis))]
    return lax.ppermute(value, axis, pairs)


def back_taps(grad_plane, weight_tap):
    flipped = jnp.transpose(weight_tap[::-1, ::-1], (0, 1, 3, 2))
    result = lax.conv_general_dilated(
        grad_plane[None],
        flipped,
        (1, 1),
        ((1, 1), (1, 1)),
        dimension_numbers=("NHWC", "HWIO", "NHWC"),
        preferred_element_type=jnp.float32,
    )
    return lax.optimization_barrier(result[0].astype(jnp.bfloat16))


def local(volume, weight, conv_bias, cotangent):
    side_cells = volume.shape[2]
    chan_in = weight.shape[3]
    chan_out = weight.shape[4]
    half_cells = side_cells // 2
    quarter_rows = side_cells // 4
    planes = extended(volume, (("space", 1),), 1)
    near_cells = planes.reshape(1, 3, side_cells, side_cells, chan_in)
    conv_out = lax.conv_general_dilated(
        near_cells,
        weight,
        (1, 1, 1),
        ((0, 0), (1, 1), (1, 1)),
        dimension_numbers=("NDHWC", "DHWIO", "NDHWC"),
        preferred_element_type=jnp.float32,
    )
    pre_act = conv_out[0, 0] + conv_bias
    sigmoid_pre = jax.nn.sigmoid(pre_act)
    activation = pre_act * sigmoid_pre
    windows = activation.reshape(half_cells, 2, half_cells, 2, chan_out)
    exp_act = jnp.exp(windows)
    numerator = jnp.sum(exp_act * windows, axis=(1, 3))
    denominator = jnp.sum(exp_act, axis=(1, 3))
    parity = lax.axis_index("space") % 2
    partner_half = 1 - parity

    def rows_of(table, which):
        return lax.dynamic_slice_in_dim(table, which * quarter_rows, quarter_rows, 0)

    def whole_rows(mine, theirs):
        table = jnp.zeros((half_cells, half_cells, chan_out), jnp.float32)
        table = lax.dynamic_update_slice_in_dim(table, mine, parity * quarter_rows, 0)
        return lax.dynamic_update_slice_in_dim(table, theirs, partner_half * quarter_rows, 0)

    upstream = cotangent[0].astype(jnp.float32)
    got_num, got_den = partner(
        (rows_of(numerator, partner_half), rows_of(denominator, partner_half)), "space", 0
    )
    total_den = rows_of(denominator, parity) + got_den
    pool_value = (rows_of(numerator, parity) + got_num) / total_den
    pooled = pool_value.astype(jnp.bfloat16)[None]
    coef_b = upstream / total_den
    coef_a = coef_b * (1.0 - pool_value)
    far_a, far_b = partner((coef_a, coef_b), "space", 0)
    full_a = whole_rows(coef_a, far_a)[:, None, :, None, :]
    full_b = whole_rows(coef_b, far_b)[:, None, :, None, :]
    grad_act = (exp_act * (full_a + full_b * windows)).reshape(side_cells, side_cells, chan_out)
    grad_pre = (grad_act * sigmoid_pre * (1.0 + pre_act * (1.0 - sigmoid_pre))).astype(jnp.bfloat16)
    grad_pre = lax.optimization_barrier(grad_pre)
    bias_part = jnp.sum(grad_pre.astype(jnp.float32), axis=(0, 1))
    padded = jnp.pad(near_cells[0], ((0, 0), (1, 1), (1, 1), (0, 0)))
    flat_grad = grad_pre.reshape(side_cells * side_cells, chan_out)
    tap_list = []
    for depth_tap in range(3):
        for row_tap in range(3):
            for col_tap in range(3):
                window = padded[
                    depth_tap, row_tap : row_tap + side_cells, col_tap : col_tap + side_cells
                ].reshape(side_cells * side_cells, chan_in)
                tap_list.append(
                    lax.dot_general(
                        window,
                        flat_grad,
                        (((0,), (0,)), ((), ())),
                        preferred_element_type=jnp.float32,
                    )
                )
    bias_block = jnp.pad(bias_part[None, None], ((0, 0), (0, chan_in - 1), (0, 0)))
    part = jnp.concatenate([jnp.stack(tap_list), bias_block], axis=0)
    total = reduced(part)
    weight_grad = total[:taps].reshape(3, 3, 3, chan_in, chan_out)
    bias_grad = total[taps, 0]
    grad_rows = grad_pre.reshape(1, 1, side_cells, side_cells * chan_out)
    grad_near = extended(grad_rows, (("space", 1),), 1)
    grad_near = grad_near.reshape(3, side_cells, side_cells, chan_out)
    term_upper = back_taps(grad_near[2], weight[0])
    term_middle = back_taps(grad_near[1], weight[1])
    term_lower = back_taps(grad_near[0], weight[2])
    summed = (
        term_upper.astype(jnp.float32)
        + term_middle.astype(jnp.float32)
        + term_lower.astype(jnp.float32)
    )
    summed = summed.reshape(side_cells, side_cells * chan_in)
    input_grad = summed.astype(jnp.bfloat16).reshape(1, 1, side_cells, side_cells * chan_in)
    return (pooled, input_grad, weight_grad, bias_grad)


def solution(mesh):
    placed = (P("sample", "space", None, None), P(), P(), P("sample", "space", None, None))
    return jax.shard_map(
        local,
        mesh=mesh,
        in_specs=placed,
        out_specs=(P("sample", "space", None, None), P("sample", "space", None, None), P(), P()),
        check_vma=False,
    )
```

```python
import jax
import jax.numpy as jnp
from jax import lax
from jax.experimental import pallas as pl
from jax.experimental.pallas import tpu as pltpu
from jax.sharding import PartitionSpec as P

MESH = pl.DeviceIdType.MESH
BF16 = jnp.bfloat16
F32 = jnp.float32
taps = 27
pieces = 28
per_kind = 14
side = 32
pairs = 16
cells = 512
loss_scale = 256.0
ring_order = (4, 3, 5, 2, 6, 1, 7)
plane_order = sorted(
    [(dx, dr) for dx in range(4) for dr in range(8) if (dx, dr) != (0, 0)],
    key=lambda d: -(min(d[0], 4 - d[0]) + min(d[1], 8 - d[1])),
)


def place():
    space = lax.axis_index("space")
    sample = lax.axis_index("sample")
    core = lax.rem(space, 2)
    z_lo = lax.rem(lax.div(space, 2), 4)
    y = lax.div(space, 8)
    z = lax.div(sample, 4) * 4 + z_lo
    x = lax.rem(sample, 4)
    return x, y, z, core


def ident(x, y, z, core):
    return ((y * 4 + lax.rem(z, 4)) * 2 + core, lax.div(z, 4) * 4 + x)


class Reduce:
    def __init__(self):
        self.x, self.y, self.z, self.core = place()
        x, y, z = self.x, self.y, self.z
        self.kind_a = x < 2
        self.ring_at = jnp.where(self.kind_a, z, y)
        self.row_at = jnp.where(self.kind_a, y, z)
        spot = lax.rem(x, 2) * 8 + self.row_at
        self.owner = spot < per_kind
        self.kind = jnp.where(self.kind_a, 0, 1)
        self.piece = jnp.minimum(self.kind * per_kind + spot, pieces - 1)
        self.slot = x * 8 + self.row_at
        self.partner = ident(x, y, z, 1 - self.core)
        plane = lax.axis_index("space")
        far_plane = plane + 2 * self.core - 1
        self.far_exists = jnp.logical_and(far_plane >= 0, far_plane < lax.axis_size("space"))
        self.far = (jnp.clip(far_plane, 0, lax.axis_size("space") - 1), lax.axis_index("sample"))
        self.near_tap = 2 - 2 * self.core
        self.far_tap = 2 * self.core

    def plane_peer(self, dx, dr):
        row = lax.rem(self.row_at + dr, 8)
        y = jnp.where(self.kind_a, row, self.y)
        z = jnp.where(self.kind_a, self.z, row)
        return ident(lax.rem(self.x + dx, 4), y, z, self.core)

    def ring_peer(self, dr):
        at = lax.rem(self.ring_at + dr, 8)
        y = jnp.where(self.kind_a, self.y, at)
        z = jnp.where(self.kind_a, at, self.z)
        return ident(self.x, y, z, self.core)

    def owner_of(self, piece):
        kind, spot = divmod(piece, per_kind)
        x = 2 * kind + spot // 8
        row = spot % 8
        if kind == 0:
            return ident(x, row, self.z, self.core), self.x * 8 + self.y
        return ident(x, self.y, row, self.core), self.x * 8 + self.z


def signal(sem, who):
    pl.semaphore_signal(sem, inc=1, device_id=who, device_id_type=MESH)


def remote(src, dst, send, recv, who):
    return pltpu.make_async_remote_copy(
        src_ref=src, dst_ref=dst, send_sem=send, recv_sem=recv, device_id=who, device_id_type=MESH
    )


def local(src, dst, sem):
    return pltpu.make_async_copy(src, dst, sem)


def lay_weights(wraw, wf, wb):
    none = jnp.zeros((64, 128), BF16)
    for a in range(3):
        for b in range(3):
            t0, t1, t2 = (wraw[a, b, c] for c in range(3))
            for cell, column in enumerate(((t1, t2, none, t0), (t0, t1, t2, none))):
                for k, block in enumerate(column):
                    wf[a, 256 * b + 64 * k : 256 * b + 64 * k + 64, 128 * cell : 128 * cell + 128] = block
            for cell, row in enumerate(((t2, t1, t0, none), (none, t2, t1, t0))):
                at = (2 * a + cell) * 64
                for j, block in enumerate(row):
                    wb[b, at : at + 64, 128 * j : 128 * j + 128] = block


def lay_plane(xin, xk, p):
    width = 512
    row = lax.broadcasted_iota(jnp.int32, (side, width), 0)
    low = lax.rem(lax.broadcasted_iota(jnp.int32, (side, width), 1), 128) < 64
    first, last = row == 0, row == side - 1
    for chunk in range(4):
        at = width * chunk
        left = xin[p, :, at : at + width].astype(F32)
        here = xin[p, :, at + 128 : at + 128 + width].astype(F32)
        right = xin[p, :, at + 256 : at + 256 + width].astype(F32)
        beside = jnp.where(low, right, left)
        for k, value in enumerate((here, beside)):
            up = jnp.where(first, 0.0, pltpu.roll(value, 1, 0))
            down = jnp.where(last, 0.0, pltpu.roll(value, side - 1, 0))
            for b, shifted in enumerate((up, value, down)):
                shifted = shifted.astype(BF16)
                for i in range(4):
                    q = 4 * chunk + i
                    lane = 256 * b + 128 * k
                    xk[p, side * q : side * q + side, lane : lane + 128] = shifted[:, 128 * i : 128 * i + 128]


def flip_plane(xk, xt, p):
    xt[p] = xk[p, :, 256:512].T


def block_kernel(
    volume_ref, weight_ref, bias_ref, cot_ref,
    pooled_ref, input_grad_ref, total_ref,
    xin, wraw, cots, wf, wb, xk, xt, pre, act, pe, sum_e, sum_n, sums, psums, ctab, pvt, fa, fb, gs, part, bt, in_bt,
    mine, theirs, rows, rs, ring_src, ring, final, gath,
    load_sem, halo_send, halo_recv, cot_send, cot_recv, pool_send, pool_recv, bt_send, bt_recv,
    core_send, core_recv, rs_send, rs_recv, ring_send, ring_recv, ag_send, ag_recv, fw_send, fw_recv,
):
    r = Reduce()
    core = r.core
    near, far = r.near_tap, r.far_tap
    body_lanes = pl.ds(128, 2048)
    loads = [
        local(volume_ref.at[0, 0], xin.at[1, :, body_lanes], load_sem.at[0]),
        local(cot_ref.at[0], cots.at[core], load_sem.at[1]),
        local(weight_ref, wraw, load_sem.at[2]),
    ]
    for cp in loads:
        cp.start()
    bar = pltpu.get_barrier_semaphore()

    @pl.when(r.owner)
    def _():
        for dx, dr in plane_order:
            signal(bar, r.plane_peer(dx, dr))

    @pl.when(r.far_exists)
    def _():
        signal(bar, r.far)

    @pl.when(r.owner)
    def _():
        for dr in ring_order:
            signal(bar, r.ring_peer(dr))

    signal(bar, r.partner)
    for p in range(3):
        xin[p, :, 0:128] = jnp.zeros((side, 128), BF16)
        xin[p, :, 2176:2304] = jnp.zeros((side, 128), BF16)

    @pl.when(jnp.logical_not(r.far_exists))
    def _():
        xin[far] = jnp.zeros((side, 2304), BF16)
        in_bt[2 - far] = jnp.zeros((cells, 128), BF16)

    for cp in loads:
        cp.wait()
    own = jnp.where(r.owner, 1, 0)
    pl.semaphore_wait(bar, pieces + 1 + 6 * own + jnp.where(r.far_exists, 1, 0))

    own_plane = xin.at[1, :, body_lanes]
    far_halo = remote(own_plane, xin.at[2 - far, :, body_lanes], halo_send.at[0], halo_recv.at[0], r.far)

    @pl.when(r.far_exists)
    def _():
        far_halo.start()

    near_halo = remote(own_plane, xin.at[2 - near, :, body_lanes], halo_send.at[1], halo_recv.at[1], r.partner)
    near_halo.start()
    cot_copy = remote(cots.at[core], cots.at[core], cot_send, cot_recv, r.partner)
    cot_copy.start()

    lay_weights(wraw, wf, wb)
    for b in range(3):
        gs[b, 0:side, :] = jnp.zeros((side, 256), BF16)
        gs[b, side + cells : 2 * side + cells, :] = jnp.zeros((side, 256), BF16)
    lay_plane(xin, xk, 1)
    flip_plane(xk, xt, 1)
    near_halo.wait_recv()
    lay_plane(xin, xk, near)
    bias = bias_ref[...].reshape(1, 128)
    bias = jnp.concatenate([bias, bias], axis=1)
    for m in range(4):
        span = pl.ds(128 * m, 128)
        pre[span] = (
            bias
            + jnp.dot(xk[1, span], wf[1], preferred_element_type=F32)
            + jnp.dot(xk[near, span], wf[near], preferred_element_type=F32)
        )
    flip_plane(xk, xt, near)
    cot_copy.wait_recv()
    for half in range(2):
        for row in range(8):
            ctab[pl.ds(8 * half + row, 16, stride=16), :] = cots[half, row].astype(F32)

    @pl.when(r.far_exists)
    def _():
        far_halo.wait_recv()

    lay_plane(xin, xk, far)
    pool_copies = []
    for m in range(4):
        span = pl.ds(128 * m, 128)
        v = pre[span] + jnp.dot(xk[far, span], wf[far], preferred_element_type=F32)
        s = 0.5 * jnp.tanh(0.5 * v) + 0.5
        z = v * s
        e = jnp.exp(z)
        act[span] = z
        pe[span] = e * (s * (1.0 + (v - z)))
        n = e * z
        sum_e[span] = e[:, :128] + e[:, 128:]
        sum_n[span] = n[:, :128] + n[:, 128:]
        half = pl.ds(64 * m, 64)
        even = pl.ds(128 * m, 64, stride=2)
        odd = pl.ds(128 * m + 1, 64, stride=2)
        sums[m, 0] = sum_e[even, :] + sum_e[odd, :]
        sums[m, 1] = sum_n[even, :] + sum_n[odd, :]
        cp = remote(sums.at[m], psums.at[m], pool_send.at[m], pool_recv.at[m], r.partner)
        cp.start()
        pool_copies.append(cp)
    flip_plane(xk, xt, far)
    row = lax.rem(lax.broadcasted_iota(jnp.int32, (128, 256), 0), side)
    bias_part = jnp.zeros((1, 256), F32)
    for m in range(4):
        pool_copies[m].wait_recv()
        den = sums[m, 0] + psums[m, 0]
        value = (sums[m, 1] + psums[m, 1]) / den
        half = pl.ds(64 * m, 64)
        pvt[half] = value
        cb = ctab[half] / den
        ca = cb * (1.0 - value)
        even = pl.ds(128 * m, 64, stride=2)
        odd = pl.ds(128 * m + 1, 64, stride=2)
        fa[even, :] = ca
        fa[odd, :] = ca
        fb[even, :] = cb
        fb[odd, :] = cb
        span = pl.ds(128 * m, 128)
        wide_a = jnp.concatenate([fa[span], fa[span]], axis=1)
        wide_b = jnp.concatenate([fb[span], fb[span]], axis=1)
        g = (pe[span] * (wide_a + wide_b * act[span])).astype(BF16)
        gs[1, side + 128 * m : side + 128 * m + 128, :] = g
        g = g.astype(F32)
        bias_part = bias_part + jnp.sum(g, axis=0, keepdims=True)
        after = jnp.where(row == side - 1, 0.0, pltpu.roll(g, 127, 0))
        before = jnp.where(row == 0, 0.0, pltpu.roll(g, 1, 0))
        gs[0, side + 128 * m : side + 128 * m + 128, :] = after.astype(BF16)
        gs[2, side + 128 * m : side + 128 * m + 128, :] = before.astype(BF16)

    half = pl.ds(pl.multiple_of(core * 32, 32), 32)
    far_half = pl.ds(pl.multiple_of(32 - core * 32, 32), 32)
    core_copies = []
    part[27] = jnp.zeros((64, 128), F32)
    part[27, 0:1, :] = bias_part[:, :128] + bias_part[:, 128:]
    for a in range(3):
        for b in range(3):
            g = a * 3 + b
            block = jnp.dot(xt[a], gs[b, side : side + cells, :], preferred_element_type=F32)
            part[3 * g] = block[192:256, :128] + block[0:64, 128:]
            part[3 * g + 1] = block[0:64, :128] + block[64:128, 128:]
            part[3 * g + 2] = block[64:128, :128] + block[128:192, 128:]
            span = pl.ds(3 * g, 3 if g < 8 else 4)
            mine[span] = part[span, far_half, :].astype(BF16)
            cp = remote(mine.at[span], theirs.at[span], core_send.at[g], core_recv.at[g], r.partner)
            cp.start()
            core_copies.append(cp)
    rs_copies = []
    for g in range(9):
        count = 3 if g < 8 else 4
        span = pl.ds(3 * g, count)
        core_copies[g].wait_recv()
        rows[span] = (part[span, half, :] + theirs[span].astype(F32)).astype(BF16)
        for piece in range(3 * g, 3 * g + count):
            who, slot = r.owner_of(piece)
            is_me = jnp.logical_and(r.owner, r.piece == piece)
            cp = remote(rows.at[piece], rs.at[slot], rs_send.at[piece], rs_recv, who)
            rs_copies.append((is_me, cp))

            @pl.when(jnp.logical_not(is_me))
            def _(cp=cp):
                cp.start()

            @pl.when(is_me)
            def _(piece=piece):
                local(rows.at[piece], rs.at[r.slot], rs_recv).start()

    for m in range(4):
        at = 128 * m
        total = jnp.zeros((128, 384), F32)
        for b in range(3):
            wide = jnp.concatenate(
                [
                    gs[b, at : at + 128, 128:256],
                    gs[b, at + 32 : at + 160, :],
                    gs[b, at + 64 : at + 192, 0:128],
                ],
                axis=1,
            )
            total = total + lax.dot_general(
                wide, wb[b], (((1,), (1,)), ((), ())), preferred_element_type=F32
            )
        for a in range(3):
            bt[a, at : at + 128, :] = total[:, 128 * a : 128 * a + 128].astype(BF16)
    bt_far = remote(bt.at[far], in_bt.at[far], bt_send.at[0], bt_recv.at[0], r.far)

    @pl.when(r.far_exists)
    def _():
        bt_far.start()

    bt_near = remote(bt.at[near], in_bt.at[near], bt_send.at[1], bt_recv.at[1], r.partner)
    bt_near.start()
    for row in range(8):
        pooled_ref[0, row] = pvt[pl.ds(8 * core + row, 16, stride=16), :].astype(BF16)

    @pl.when(r.owner)
    def _():
        local(rs, rs, rs_recv).wait()
        total = rs[0].astype(F32)
        for i in range(1, 32):
            total = total + rs[i].astype(F32)
        ring_src[...] = total.astype(BF16)
        copies = []
        for dr in ring_order:
            cp = remote(ring_src, ring.at[r.ring_at], ring_send.at[dr], ring_recv, r.ring_peer(dr))
            cp.start()
            copies.append(cp)
        local(ring_src, ring.at[r.ring_at], ring_recv).start()
        local(ring, ring, ring_recv).wait()
        total = ring[0].astype(F32)
        for i in range(1, 8):
            total = total + ring[i].astype(F32)
        final[...] = total.astype(BF16)
        for i, (dx, dr) in enumerate(plane_order):
            cp = remote(final, gath.at[core, r.piece], ag_send.at[i], ag_recv.at[r.kind], r.plane_peer(dx, dr))
            cp.start()
            copies.append(cp)
        local(final, gath.at[core, r.piece], ag_recv.at[r.kind]).start()
        for cp in copies:
            cp.wait_send()

    bt_near.wait()

    @pl.when(r.far_exists)
    def _():
        bt_far.wait()

    for q in range(pairs):
        span = pl.ds(side * q, side)
        summed = in_bt[0, span].astype(F32) + bt[1, span].astype(F32) + in_bt[2, span].astype(F32)
        input_grad_ref[0, 0, :, 128 * q : 128 * q + 128] = summed.astype(BF16)

    fw_copies = []
    for kind in range(2):
        span = gath.at[core, pl.ds(per_kind * kind, per_kind)]
        local(span, span, ag_recv.at[kind]).wait()
        cp = remote(span, span, fw_send.at[kind], fw_recv.at[kind], r.partner)
        cp.start()
        fw_copies.append(cp)
    for cp in core_copies + pool_copies + [near_halo, cot_copy]:
        cp.wait_send()

    @pl.when(r.far_exists)
    def _():
        far_halo.wait_send()

    for is_me, cp in rs_copies:

        @pl.when(jnp.logical_not(is_me))
        def _(cp=cp):
            cp.wait_send()

    for cp in fw_copies:
        cp.wait()
    for h in range(2):
        total_ref[:, 32 * h : 32 * h + 32, :] = gath[h].astype(F32) * (1.0 / loss_scale)


def block(volume, weight, conv_bias, cotangent):
    dma = pltpu.SemaphoreType.DMA
    vmem = pltpu.VMEM
    anywhere = pl.BlockSpec(memory_space=pl.ANY)
    here = pl.BlockSpec(memory_space=pltpu.VMEM)
    pooled, input_grad, total = pl.pallas_call(
        block_kernel,
        out_shape=(
            jax.ShapeDtypeStruct(cotangent.shape, BF16),
            jax.ShapeDtypeStruct(volume.shape, BF16),
            jax.ShapeDtypeStruct((pieces, 64, 128), F32),
        ),
        in_specs=[anywhere, anywhere, here, anywhere],
        out_specs=(here, here, here),
        scratch_shapes=[
            vmem((3, side, 2304), BF16),
            vmem((3, 3, 3, 64, 128), BF16),
            vmem((2, 8, 16, 128), BF16),
            vmem((3, 768, 256), BF16),
            vmem((3, 384, 512), BF16),
            vmem((3, cells, 768), BF16),
            vmem((3, 256, cells), BF16),
            vmem((cells, 256), F32),
            vmem((cells, 256), F32),
            vmem((cells, 256), F32),
            vmem((cells, 128), F32),
            vmem((cells, 128), F32),
            vmem((4, 2, 64, 128), F32),
            vmem((4, 2, 64, 128), F32),
            vmem((256, 128), F32),
            vmem((256, 128), F32),
            vmem((cells, 128), F32),
            vmem((cells, 128), F32),
            vmem((3, cells + 2 * side, 256), BF16),
            vmem((pieces, 64, 128), F32),
            vmem((3, cells, 128), BF16),
            vmem((3, cells, 128), BF16),
            vmem((pieces, 32, 128), BF16),
            vmem((pieces, 32, 128), BF16),
            vmem((pieces, 32, 128), BF16),
            vmem((32, 32, 128), BF16),
            vmem((32, 128), BF16),
            vmem((8, 32, 128), BF16),
            vmem((32, 128), BF16),
            vmem((2, pieces, 32, 128), BF16),
            dma((3,)), dma((2,)), dma((2,)), dma, dma, dma((4,)), dma((4,)), dma((2,)), dma((2,)),
            dma((9,)), dma((9,)), dma((pieces,)), dma, dma((8,)), dma, dma((31,)), dma((2,)), dma((2,)), dma((2,)),
        ],
        compiler_params=pltpu.CompilerParams(
            collective_id=0, has_side_effects=True, vmem_limit_bytes=48 * 2**20
        ),
        name="conv_block",
    )(volume, weight, conv_bias, cotangent)
    return pooled, input_grad, total[:taps].reshape(weight.shape), total[taps, 0]


def solution(mesh):
    placed = (P("sample", "space", None, None), P(), P(), P("sample", "space", None, None))
    return jax.shard_map(
        block,
        mesh=mesh,
        in_specs=placed,
        out_specs=(P("sample", "space", None, None), P("sample", "space", None, None), P(), P()),
        check_vma=False,
    )
```

```python
import jax
import jax.numpy as jnp
from jax import lax
from jax.experimental import pallas as pl
from jax.experimental.pallas import tpu as pltpu
from jax.sharding import PartitionSpec as P

MESH = pl.DeviceIdType.MESH
BF16 = jnp.bfloat16
F32 = jnp.float32
taps = 27
blocks = 28
per_piece = 1
pieces = blocks // per_piece
per_kind = pieces // 2
side = 32
pairs = 16
cells = 512
loss_scale = 256.0
plane_order = sorted(((x, row) for x in range(4) for row in range(8)), key=sum)
spots = tuple((x, row) for row in range(7) for x in range(2))


def place():
    space = lax.axis_index("space")
    sample = lax.axis_index("sample")
    core = lax.rem(space, 2)
    z_lo = lax.rem(lax.div(space, 2), 4)
    y = lax.div(space, 8)
    z = lax.div(sample, 4) * 4 + z_lo
    x = lax.rem(sample, 4)
    return x, y, z, core


def ident(x, y, z, core):
    return ((y * 4 + lax.rem(z, 4)) * 2 + core, lax.div(z, 4) * 4 + x)


class Reduce:
    def __init__(self):
        self.x, self.y, self.z, self.core = place()
        x, y, z = self.x, self.y, self.z
        self.kind_a = x < 2
        self.ring_at = jnp.where(self.kind_a, z, y)
        self.row_at = jnp.where(self.kind_a, y, z)
        self.kind = jnp.where(self.kind_a, 0, 1)
        side_x = jnp.where(self.kind_a, x, 3 - x)
        self.owner = False
        self.piece = 0
        for i, (sx, row) in enumerate(spots):
            here = jnp.logical_and(side_x == sx, self.row_at == row)
            self.owner = jnp.logical_or(self.owner, here)
            self.piece = self.piece + jnp.where(here, i, 0)
        self.piece = self.piece + self.kind * per_kind
        self.slot = x * 8 + self.row_at
        self.partner = ident(x, y, z, 1 - self.core)
        plane = lax.axis_index("space")
        far_plane = plane + 2 * self.core - 1
        self.far_exists = jnp.logical_and(far_plane >= 0, far_plane < lax.axis_size("space"))
        self.far = (jnp.clip(far_plane, 0, lax.axis_size("space") - 1), lax.axis_index("sample"))
        self.near_tap = 2 - 2 * self.core
        self.far_tap = 2 * self.core

    def plane_peer(self, x, row):
        y = jnp.where(self.kind_a, row, self.y)
        z = jnp.where(self.kind_a, self.z, row)
        return ident(x, y, z, self.core), jnp.logical_and(self.x == x, self.row_at == row)

    def ring_peer(self, at):
        y = jnp.where(self.kind_a, self.y, at)
        z = jnp.where(self.kind_a, at, self.z)
        return ident(self.x, y, z, self.core), self.ring_at == at

    def owner_of(self, piece):
        kind, i = divmod(piece, per_kind)
        x, row = spots[i]
        if kind == 0:
            return ident(x, row, self.z, self.core), self.x * 8 + self.y
        return ident(3 - x, self.y, row, self.core), self.x * 8 + self.z


def unless(me, action, otherwise=None):
    pl.when(jnp.logical_not(me))(action)
    if otherwise is not None:
        pl.when(me)(otherwise)


def signal(sem, who):
    pl.semaphore_signal(sem, inc=1, device_id=who, device_id_type=MESH)


def remote(src, dst, send, recv, who):
    return pltpu.make_async_remote_copy(
        src_ref=src, dst_ref=dst, send_sem=send, recv_sem=recv, device_id=who, device_id_type=MESH
    )


def local(src, dst, sem):
    return pltpu.make_async_copy(src, dst, sem)


def lay_weights(wraw, wf, wb):
    none = jnp.zeros((64, 128), BF16)
    for a in range(3):
        for b in range(3):
            t0, t1, t2 = (wraw[a, b, c] for c in range(3))
            for cell, column in enumerate(((t1, t2, none, t0), (t0, t1, t2, none))):
                for k, block in enumerate(column):
                    wf[a, 256 * b + 64 * k : 256 * b + 64 * k + 64, 128 * cell : 128 * cell + 128] = block
            for cell, row in enumerate(((t2, t1, t0, none), (none, t2, t1, t0))):
                at = (2 * a + cell) * 64
                for j, block in enumerate(row):
                    wb[b, at : at + 64, 128 * j : 128 * j + 128] = block


def lay_plane(xin, xk, p):
    width = 512
    row = lax.broadcasted_iota(jnp.int32, (side, width), 0)
    low = lax.rem(lax.broadcasted_iota(jnp.int32, (side, width), 1), 128) < 64
    first, last = row == 0, row == side - 1
    for chunk in range(4):
        at = width * chunk
        left = xin[p, :, at : at + width].astype(F32)
        here = xin[p, :, at + 128 : at + 128 + width].astype(F32)
        right = xin[p, :, at + 256 : at + 256 + width].astype(F32)
        beside = jnp.where(low, right, left)
        for k, value in enumerate((here, beside)):
            up = jnp.where(first, 0.0, pltpu.roll(value, 1, 0))
            down = jnp.where(last, 0.0, pltpu.roll(value, side - 1, 0))
            for b, shifted in enumerate((up, value, down)):
                shifted = shifted.astype(BF16)
                for i in range(4):
                    q = 4 * chunk + i
                    lane = 256 * b + 128 * k
                    xk[p, side * q : side * q + side, lane : lane + 128] = shifted[:, 128 * i : 128 * i + 128]


def flip_plane(xk, xt, p):
    xt[p] = xk[p, :, 256:512].T


def block_kernel(
    volume_ref, weight_ref, bias_hbm, cot_ref,
    pooled_ref, input_grad_ref, weight_grad_ref, bias_grad_ref,
    xin, wraw, bias_ref, cots, wf, wb, xk, xt, pre, act, pe, sum_e, sum_n, sums, psums, ctab, pvt, fa, fb, gs, part, bt, in_bt,
    mine, theirs, rows, rs, ring_src, ring, final,
    gath, pooled_out, input_grad_out, weights, bias_out,
    load_sem, halo_send, halo_recv, cot_send, cot_recv, pool_send, pool_recv, bt_send, bt_recv,
    core_send, core_recv, rs_send, rs_recv, ring_send, ring_recv, ag_send, ag_recv, fw_send, fw_recv, out_sem,
):
    r = Reduce()
    core = r.core
    near, far = r.near_tap, r.far_tap
    body_lanes = pl.ds(128, 2048)
    bar = pltpu.get_barrier_semaphore()

    @pl.when(r.far_exists)
    def _():
        signal(bar, r.far)

    signal(bar, r.partner)
    loads = [
        local(volume_ref.at[0, 0], xin.at[1, :, body_lanes], load_sem.at[0]),
        local(cot_ref.at[0], cots.at[core], load_sem.at[1]),
        local(weight_ref, wraw, load_sem.at[2]),
        local(bias_hbm, bias_ref, load_sem.at[3]),
    ]
    for cp in loads:
        cp.start()

    @pl.when(r.owner)
    def _():
        for x, row in reversed(plane_order):
            who, me = r.plane_peer(x, row)
            unless(me, lambda who=who: signal(bar, who))
        for at in range(8):
            who, me = r.ring_peer(at)
            unless(me, lambda who=who: signal(bar, who))

    for p in range(3):
        xin[p, :, 0:128] = jnp.zeros((side, 128), BF16)
        xin[p, :, 2176:2304] = jnp.zeros((side, 128), BF16)

    @pl.when(jnp.logical_not(r.far_exists))
    def _():
        xin[far] = jnp.zeros((side, 2304), BF16)
        in_bt[2 - far] = jnp.zeros((cells, 128), BF16)

    for cp in loads:
        cp.wait()
    own = jnp.where(r.owner, 1, 0)
    pl.semaphore_wait(bar, pieces + 1 + 6 * own + jnp.where(r.far_exists, 1, 0))

    own_plane = xin.at[1, :, body_lanes]
    far_halo = remote(own_plane, xin.at[2 - far, :, body_lanes], halo_send.at[0], halo_recv.at[0], r.far)

    @pl.when(r.far_exists)
    def _():
        far_halo.start()

    near_halo = remote(own_plane, xin.at[2 - near, :, body_lanes], halo_send.at[1], halo_recv.at[1], r.partner)
    near_halo.start()
    cot_copy = remote(cots.at[core], cots.at[core], cot_send, cot_recv, r.partner)
    cot_copy.start()

    lay_weights(wraw, wf, wb)
    for b in range(3):
        gs[b, 0:side, :] = jnp.zeros((side, 256), BF16)
        gs[b, side + cells : 2 * side + cells, :] = jnp.zeros((side, 256), BF16)
    lay_plane(xin, xk, 1)
    flip_plane(xk, xt, 1)
    near_halo.wait_recv()
    lay_plane(xin, xk, near)
    bias = bias_ref[...].reshape(1, 128)
    bias = jnp.concatenate([bias, bias], axis=1)
    for m in range(4):
        span = pl.ds(128 * m, 128)
        pre[span] = (
            bias
            + jnp.dot(xk[1, span], wf[1], preferred_element_type=F32)
            + jnp.dot(xk[near, span], wf[near], preferred_element_type=F32)
        )
    flip_plane(xk, xt, near)
    cot_copy.wait_recv()
    for half in range(2):
        for row in range(8):
            ctab[pl.ds(8 * half + row, 16, stride=16), :] = cots[half, row].astype(F32)

    @pl.when(r.far_exists)
    def _():
        far_halo.wait_recv()

    lay_plane(xin, xk, far)
    pool_copies = []
    for m in range(4):
        span = pl.ds(128 * m, 128)
        v = pre[span] + jnp.dot(xk[far, span], wf[far], preferred_element_type=F32)
        s = 0.5 * jnp.tanh(0.5 * v) + 0.5
        z = v * s
        e = jnp.exp(z)
        act[span] = z
        pe[span] = e * (s * (1.0 + (v - z)))
        n = e * z
        sum_e[span] = e[:, :128] + e[:, 128:]
        sum_n[span] = n[:, :128] + n[:, 128:]
        half = pl.ds(64 * m, 64)
        even = pl.ds(128 * m, 64, stride=2)
        odd = pl.ds(128 * m + 1, 64, stride=2)
        sums[m, 0] = sum_e[even, :] + sum_e[odd, :]
        sums[m, 1] = sum_n[even, :] + sum_n[odd, :]
        cp = remote(sums.at[m], psums.at[m], pool_send.at[m], pool_recv.at[m], r.partner)
        cp.start()
        pool_copies.append(cp)
    flip_plane(xk, xt, far)
    row = lax.rem(lax.broadcasted_iota(jnp.int32, (128, 256), 0), side)
    bias_part = jnp.zeros((1, 256), F32)
    for m in range(4):
        pool_copies[m].wait_recv()
        den = sums[m, 0] + psums[m, 0]
        value = (sums[m, 1] + psums[m, 1]) / den
        half = pl.ds(64 * m, 64)
        pvt[half] = value
        cb = ctab[half] / den
        ca = cb * (1.0 - value)
        even = pl.ds(128 * m, 64, stride=2)
        odd = pl.ds(128 * m + 1, 64, stride=2)
        fa[even, :] = ca
        fa[odd, :] = ca
        fb[even, :] = cb
        fb[odd, :] = cb
        span = pl.ds(128 * m, 128)
        wide_a = jnp.concatenate([fa[span], fa[span]], axis=1)
        wide_b = jnp.concatenate([fb[span], fb[span]], axis=1)
        g = (pe[span] * (wide_a + wide_b * act[span])).astype(BF16)
        gs[1, side + 128 * m : side + 128 * m + 128, :] = g
        g = g.astype(F32)
        bias_part = bias_part + jnp.sum(g, axis=0, keepdims=True)
        after = jnp.where(row == side - 1, 0.0, pltpu.roll(g, 127, 0))
        before = jnp.where(row == 0, 0.0, pltpu.roll(g, 1, 0))
        gs[0, side + 128 * m : side + 128 * m + 128, :] = after.astype(BF16)
        gs[2, side + 128 * m : side + 128 * m + 128, :] = before.astype(BF16)

    half = pl.ds(pl.multiple_of(core * 32, 32), 32)
    far_half = pl.ds(pl.multiple_of(32 - core * 32, 32), 32)
    core_copies = []
    part[27] = jnp.zeros((64, 128), F32)
    part[27, 0:1, :] = bias_part[:, :128] + bias_part[:, 128:]
    for a in range(3):
        for b in range(3):
            g = a * 3 + b
            block = jnp.dot(xt[a], gs[b, side : side + cells, :], preferred_element_type=F32)
            part[3 * g] = block[192:256, :128] + block[0:64, 128:]
            part[3 * g + 1] = block[0:64, :128] + block[64:128, 128:]
            part[3 * g + 2] = block[64:128, :128] + block[128:192, 128:]
            span = pl.ds(3 * g, 3 if g < 8 else 4)
            mine[span] = part[span, far_half, :].astype(BF16)
            cp = remote(mine.at[span], theirs.at[span], core_send.at[g], core_recv.at[g], r.partner)
            cp.start()
            core_copies.append(cp)
    rs_copies = []
    sent = 0
    for g in range(9):
        count = 3 if g < 8 else 4
        span = pl.ds(3 * g, count)
        core_copies[g].wait_recv()
        rows[span] = (part[span, half, :] + theirs[span].astype(F32)).astype(BF16)
        while sent < pieces and per_piece * (sent + 1) <= 3 * g + count:
            who, slot = r.owner_of(sent)
            is_me = jnp.logical_and(r.owner, r.piece == sent)
            taps_of = rows.at[pl.ds(per_piece * sent, per_piece)]
            cp = remote(taps_of, rs.at[slot], rs_send.at[sent], rs_recv, who)
            keep = local(taps_of, rs.at[r.slot], rs_recv)
            unless(is_me, cp.start, keep.start)
            rs_copies.append((is_me, cp))
            sent += 1

    for m in range(4):
        at = 128 * m
        total = jnp.zeros((128, 384), F32)
        for b in range(3):
            wide = jnp.concatenate(
                [
                    gs[b, at : at + 128, 128:256],
                    gs[b, at + 32 : at + 160, :],
                    gs[b, at + 64 : at + 192, 0:128],
                ],
                axis=1,
            )
            total = total + lax.dot_general(
                wide, wb[b], (((1,), (1,)), ((), ())), preferred_element_type=F32
            )
        for a in range(3):
            bt[a, at : at + 128, :] = total[:, 128 * a : 128 * a + 128].astype(BF16)
    bt_far = remote(bt.at[far], in_bt.at[far], bt_send.at[0], bt_recv.at[0], r.far)

    @pl.when(r.far_exists)
    def _():
        bt_far.start()

    bt_near = remote(bt.at[near], in_bt.at[near], bt_send.at[1], bt_recv.at[1], r.partner)
    bt_near.start()
    for row in range(8):
        pooled_out[row] = pvt[pl.ds(8 * core + row, 16, stride=16), :].astype(BF16)

    outs = [local(pooled_out, pooled_ref.at[0], out_sem.at[0])]
    outs[0].start()
    @pl.when(r.owner)
    def _():
        local(rs, rs, rs_recv).wait()
        total = rs[0].astype(F32)
        for i in range(1, 32):
            total = total + rs[i].astype(F32)
        ring_src[...] = total.astype(BF16)
        ring_copies = []
        for at in range(8):
            who, me = r.ring_peer(at)
            cp = remote(ring_src, ring.at[r.ring_at], ring_send.at[at], ring_recv, who)
            unless(me, cp.start, local(ring_src, ring.at[r.ring_at], ring_recv).start)
            ring_copies.append((me, cp))
        local(ring, ring, ring_recv).wait()
        total = ring[0].astype(F32)
        for i in range(1, 8):
            total = total + ring[i].astype(F32)
        final[...] = total.astype(BF16)
        place_of = gath.at[core, pl.ds(per_piece * r.piece, per_piece)]
        for i, (x, row) in enumerate(plane_order):
            who, me = r.plane_peer(x, row)
            cp = remote(final, place_of, ag_send.at[i], ag_recv.at[r.kind], who)
            unless(me, cp.start, local(final, place_of, ag_recv.at[r.kind]).start)
            ring_copies.append((me, cp))
        for me, cp in ring_copies:
            unless(me, cp.wait_send)

    bt_near.wait()

    @pl.when(r.far_exists)
    def _():
        bt_far.wait()

    for q in range(pairs):
        span = pl.ds(side * q, side)
        summed = in_bt[0, span].astype(F32) + bt[1, span].astype(F32) + in_bt[2, span].astype(F32)
        input_grad_out[:, 128 * q : 128 * q + 128] = summed.astype(BF16)
    outs.append(local(input_grad_out, input_grad_ref.at[0, 0], out_sem.at[1]))
    outs[1].start()

    fw_copies = []
    for kind in range(2):
        span = gath.at[core, pl.ds(blocks // 2 * kind, blocks // 2)]
        local(span, span, ag_recv.at[kind]).wait()
        cp = remote(span, span, fw_send.at[kind], fw_recv.at[kind], r.partner)
        cp.start()
        fw_copies.append(cp)
    for cp in core_copies + pool_copies + [near_halo, cot_copy]:
        cp.wait_send()

    @pl.when(r.far_exists)
    def _():
        far_halo.wait_send()

    for is_me, cp in rs_copies:
        unless(is_me, cp.wait_send)
    for kind in range(2):
        fw_copies[kind].wait()
        first, last = blocks // 2 * kind, min(blocks // 2 * (kind + 1), taps)
        for h in range(2):
            value = gath[h, first:last].astype(F32) * (1.0 / loss_scale)
            weights[first:last, 32 * h : 32 * h + 32, :] = value
        span = pl.ds(first, last - first)
        outs.append(local(weights.at[span], weight_grad_ref.at[span], out_sem.at[2 + kind]))
        outs[-1].start()
    bias_out[...] = gath[0, taps, 0, :].astype(F32) * (1.0 / loss_scale)
    outs.append(local(bias_out, bias_grad_ref, out_sem.at[4]))
    outs[-1].start()
    for cp in outs:
        cp.wait()


def hand_over(pooled, input_grad, weight_grad, bias_grad, pooled_ref, input_grad_ref, weight_ref, bias_ref, w, g, p, b, get, put):
    moves = [(weight_grad.at[pl.ds(9 * i, 9)], w.at[pl.ds(9 * i, 9)], weight_ref.at[pl.ds(9 * i, 9)]) for i in range(3)]
    moves += [(input_grad, g, input_grad_ref), (pooled, p, pooled_ref), (bias_grad, b, bias_ref)]
    reads = [local(src, mid, get.at[i]) for i, (src, mid, dst) in enumerate(moves)]
    writes = [local(mid, dst, put.at[i]) for i, (src, mid, dst) in enumerate(moves)]
    for cp in reads:
        cp.start()
    for arrive, leave in zip(reads, writes):
        arrive.wait()
        leave.start()
    for cp in writes:
        cp.wait()


def block(volume, weight, conv_bias, cotangent):
    dma = pltpu.SemaphoreType.DMA
    vmem = pltpu.VMEM
    anywhere = pl.BlockSpec(memory_space=pltpu.HBM)
    shapes = (
        jax.ShapeDtypeStruct(cotangent.shape, BF16),
        jax.ShapeDtypeStruct(volume.shape, BF16),
        jax.ShapeDtypeStruct((taps, 64, 128), F32),
        jax.ShapeDtypeStruct(conv_bias.shape, F32),
    )
    results = pl.pallas_call(
        block_kernel,
        out_shape=shapes,
        in_specs=[anywhere, anywhere, anywhere, anywhere],
        out_specs=(anywhere,) * 4,
        scratch_shapes=[
            vmem((3, side, 2304), BF16),
            vmem((3, 3, 3, 64, 128), BF16),
            vmem((128,), F32),
            vmem((2, 8, 16, 128), BF16),
            vmem((3, 768, 256), BF16),
            vmem((3, 384, 512), BF16),
            vmem((3, cells, 768), BF16),
            vmem((3, 256, cells), BF16),
            vmem((cells, 256), F32),
            vmem((cells, 256), F32),
            vmem((cells, 256), F32),
            vmem((cells, 128), F32),
            vmem((cells, 128), F32),
            vmem((4, 2, 64, 128), F32),
            vmem((4, 2, 64, 128), F32),
            vmem((256, 128), F32),
            vmem((256, 128), F32),
            vmem((cells, 128), F32),
            vmem((cells, 128), F32),
            vmem((3, cells + 2 * side, 256), BF16),
            vmem((blocks, 64, 128), F32),
            vmem((3, cells, 128), BF16),
            vmem((3, cells, 128), BF16),
            vmem((blocks, 32, 128), BF16),
            vmem((blocks, 32, 128), BF16),
            vmem((blocks, 32, 128), BF16),
            vmem((32, per_piece, 32, 128), BF16),
            vmem((per_piece, 32, 128), BF16),
            vmem((8, per_piece, 32, 128), BF16),
            vmem((per_piece, 32, 128), BF16),
            vmem((2, blocks, 32, 128), BF16),
            vmem((8, 16, 128), BF16),
            vmem((side, 2048), BF16),
            vmem((taps, 64, 128), F32),
            vmem((128,), F32),
            dma((4,)), dma((2,)), dma((2,)), dma, dma, dma((4,)), dma((4,)), dma((2,)), dma((2,)),
            dma((9,)), dma((9,)), dma((pieces,)), dma, dma((8,)), dma, dma((32,)), dma((2,)), dma((2,)), dma((2,)), dma((6,)),
        ],
        compiler_params=pltpu.CompilerParams(
            collective_id=0, has_side_effects=True, vmem_limit_bytes=62 * 2**20
        ),
        name="conv_block",
    )(volume, weight, conv_bias, cotangent)
    pooled, input_grad, weight_grad, bias_grad = pl.pallas_call(
        hand_over,
        out_shape=shapes,
        in_specs=[anywhere] * 4,
        out_specs=(anywhere,) * 4,
        scratch_shapes=[vmem(v.shape, v.dtype) for v in (shapes[2], shapes[1], shapes[0], shapes[3])] + [dma((6,)), dma((6,))],
        compiler_params=pltpu.CompilerParams(vmem_limit_bytes=62 * 2**20),
        name="hand_over",
    )(*results)
    return pooled, input_grad, weight_grad.reshape(weight.shape), bias_grad


def solution(mesh):
    placed = (P("sample", "space", None, None), P(), P(), P("sample", "space", None, None))
    return jax.shard_map(
        block,
        mesh=mesh,
        in_specs=placed,
        out_specs=(P("sample", "space", None, None), P("sample", "space", None, None), P(), P()),
        check_vma=False,
    )
```

```python
import jax
import jax.numpy as jnp
from jax import lax
from jax.experimental import pallas as pl
from jax.experimental.pallas import tpu as pltpu
from jax.sharding import PartitionSpec as P

MESH = pl.DeviceIdType.MESH
BF16 = jnp.bfloat16
F32 = jnp.float32
taps = 27
blocks = 28
per_piece = 1
pieces = blocks // per_piece
per_kind = pieces // 2
side = 32
pairs = 16
cells = 512
loss_scale = 256.0
spots = tuple((x, row) for row in range(7) for x in range(2))


def place():
    space = lax.axis_index("space")
    sample = lax.axis_index("sample")
    core = lax.rem(space, 2)
    z_lo = lax.rem(lax.div(space, 2), 4)
    y = lax.div(space, 8)
    z = lax.div(sample, 4) * 4 + z_lo
    x = lax.rem(sample, 4)
    return x, y, z, core


def ident(x, y, z, core):
    return ((y * 4 + lax.rem(z, 4)) * 2 + core, lax.div(z, 4) * 4 + x)


class Reduce:
    def __init__(self):
        self.x, self.y, self.z, self.core = place()
        x, y, z = self.x, self.y, self.z
        self.kind_a = x < 2
        self.ring_at = jnp.where(self.kind_a, z, y)
        self.row_at = jnp.where(self.kind_a, y, z)
        self.kind = jnp.where(self.kind_a, 0, 1)
        side_x = jnp.where(self.kind_a, x, 3 - x)
        self.owner = False
        self.piece = 0
        for i, (sx, row) in enumerate(spots):
            here = jnp.logical_and(side_x == sx, self.row_at == row)
            self.owner = jnp.logical_or(self.owner, here)
            self.piece = self.piece + jnp.where(here, i, 0)
        self.piece = self.piece + self.kind * per_kind
        self.slot = x * 8 + self.row_at
        self.partner = ident(x, y, z, 1 - self.core)
        plane = lax.axis_index("space")
        far_plane = plane + 2 * self.core - 1
        self.far_exists = jnp.logical_and(far_plane >= 0, far_plane < lax.axis_size("space"))
        self.far = (jnp.clip(far_plane, 0, lax.axis_size("space") - 1), lax.axis_index("sample"))
        self.near_tap = 2 - 2 * self.core
        self.far_tap = 2 * self.core

    def plane_peer(self, i):
        at = i + jnp.where(i >= self.row_at * 4 + self.x, 1, 0)
        row = lax.div(at, 4)
        y = jnp.where(self.kind_a, row, self.y)
        z = jnp.where(self.kind_a, self.z, row)
        return ident(lax.rem(at, 4), y, z, self.core)

    def ring_peer(self, i):
        at = i + jnp.where(i >= self.ring_at, 1, 0)
        y = jnp.where(self.kind_a, self.y, at)
        z = jnp.where(self.kind_a, at, self.z)
        return ident(self.x, y, z, self.core)

    def owner_of(self, piece):
        kind, i = divmod(piece, per_kind)
        x, row = spots[i]
        if kind == 0:
            return ident(x, row, self.z, self.core), self.x * 8 + self.y
        return ident(3 - x, self.y, row, self.core), self.x * 8 + self.z


def unless(me, action, otherwise=None):
    pl.when(jnp.logical_not(me))(action)
    if otherwise is not None:
        pl.when(me)(otherwise)


def signal(sem, who):
    pl.semaphore_signal(sem, inc=1, device_id=who, device_id_type=MESH)


def remote(src, dst, send, recv, who):
    return pltpu.make_async_remote_copy(
        src_ref=src, dst_ref=dst, send_sem=send, recv_sem=recv, device_id=who, device_id_type=MESH
    )


def local(src, dst, sem):
    return pltpu.make_async_copy(src, dst, sem)


def lay_weights(wraw, wf, wb):
    none = jnp.zeros((64, 128), BF16)
    for a in range(3):
        for b in range(3):
            t0, t1, t2 = (wraw[a, b, c] for c in range(3))
            for cell, column in enumerate(((t1, t2, none, t0), (t0, t1, t2, none))):
                for k, block in enumerate(column):
                    wf[a, 256 * b + 64 * k : 256 * b + 64 * k + 64, 128 * cell : 128 * cell + 128] = block
            for cell, row in enumerate(((t2, t1, t0, none), (none, t2, t1, t0))):
                at = (2 * a + cell) * 64
                for j, block in enumerate(row):
                    wb[b, at : at + 64, 128 * j : 128 * j + 128] = block


def lay_plane(xin, xk, p, chunks=range(4)):
    width = 512
    row = lax.broadcasted_iota(jnp.int32, (side, width), 0)
    low = lax.rem(lax.broadcasted_iota(jnp.int32, (side, width), 1), 128) < 64
    first, last = row == 0, row == side - 1
    for chunk in chunks:
        at = width * chunk
        left = xin[p, :, at : at + width].astype(F32)
        here = xin[p, :, at + 128 : at + 128 + width].astype(F32)
        right = xin[p, :, at + 256 : at + 256 + width].astype(F32)
        beside = jnp.where(low, right, left)
        for k, value in enumerate((here, beside)):
            up = jnp.where(first, 0.0, pltpu.roll(value, 1, 0))
            down = jnp.where(last, 0.0, pltpu.roll(value, side - 1, 0))
            for b, shifted in enumerate((up, value, down)):
                shifted = shifted.astype(BF16)
                for i in range(4):
                    q = 4 * chunk + i
                    lane = 256 * b + 128 * k
                    xk[p, side * q : side * q + side, lane : lane + 128] = shifted[:, 128 * i : 128 * i + 128]


def flip_plane(xk, xt, p):
    xt[p] = xk[p, :, 256:512].T


def block_kernel(
    volume_ref, weight_ref, bias_hbm, cot_ref,
    pooled_ref, input_grad_ref, sum_ref,
    xin, wraw, bias_ref, cots, wf, wb, xk, xt, pre, act, pe, sum_e, sum_n, sums, psums, ctab, pvt, fa, fb, gs, part, bt, in_bt,
    mine, theirs, rows, rs, ring_src, ring, final,
    gath, pooled_out, input_grad_out,
    load_sem, halo_send, halo_recv, cot_send, cot_recv, pool_send, pool_recv, bt_send, bt_recv,
    core_send, core_recv, rs_send, rs_recv, ring_send, ring_recv, ag_send, ag_recv, fw_send, fw_recv, out_sem,
):
    r = Reduce()
    core = r.core
    near, far = r.near_tap, r.far_tap
    body_lanes = pl.ds(128, 2048)
    bar = pltpu.get_barrier_semaphore()

    @pl.when(r.far_exists)
    def _():
        signal(bar, r.far)

    signal(bar, r.partner)
    loads = [
        local(volume_ref.at[0, 0], xin.at[1, :, body_lanes], load_sem.at[0]),
        local(cot_ref.at[0], cots.at[core], load_sem.at[1]),
        local(weight_ref, wraw, load_sem.at[2]),
        local(bias_hbm, bias_ref, load_sem.at[3]),
    ]
    for cp in loads:
        cp.start()

    @pl.when(r.owner)
    def _():
        for i in reversed(range(31)):
            signal(bar, r.plane_peer(i))
        for i in range(7):
            signal(bar, r.ring_peer(i))

    for p in range(3):
        xin[p, :, 0:128] = jnp.zeros((side, 128), BF16)
        xin[p, :, 2176:2304] = jnp.zeros((side, 128), BF16)

    @pl.when(jnp.logical_not(r.far_exists))
    def _():
        xin[far] = jnp.zeros((side, 2304), BF16)
        in_bt[2 - far] = jnp.zeros((cells, 128), BF16)

    for cp in loads:
        cp.wait()
    own = jnp.where(r.owner, 1, 0)
    pl.semaphore_wait(bar, pieces + 1 + 6 * own + jnp.where(r.far_exists, 1, 0))

    own_plane = xin.at[1, :, body_lanes]
    far_halos = []
    for i, lanes in enumerate((pl.ds(128, 9 * 128), pl.ds(10 * 128, 7 * 128))):
        src = xin.at[1, :, lanes]
        far_halos.append(remote(src, xin.at[2 - far, :, lanes], halo_send.at[2 * i], halo_recv.at[2 * i], r.far))

    @pl.when(r.far_exists)
    def _():
        for cp in far_halos:
            cp.start()

    near_halo = remote(own_plane, xin.at[2 - near, :, body_lanes], halo_send.at[1], halo_recv.at[1], r.partner)
    near_halo.start()
    cot_copy = remote(cots.at[core], cots.at[core], cot_send, cot_recv, r.partner)
    cot_copy.start()

    lay_weights(wraw, wf, wb)
    for b in range(3):
        gs[b, 0:side, :] = jnp.zeros((side, 256), BF16)
        gs[b, side + cells : 2 * side + cells, :] = jnp.zeros((side, 256), BF16)
    lay_plane(xin, xk, 1)
    flip_plane(xk, xt, 1)
    near_halo.wait_recv()
    lay_plane(xin, xk, near)
    bias = bias_ref[...].reshape(1, 128)
    bias = jnp.concatenate([bias, bias], axis=1)
    for m in range(2):
        span = pl.ds(256 * m, 256)
        pre[span] = (
            bias
            + jnp.dot(xk[1, span], wf[1], preferred_element_type=F32)
            + jnp.dot(xk[near, span], wf[near], preferred_element_type=F32)
        )
    flip_plane(xk, xt, near)
    cot_copy.wait_recv()
    for half in range(2):
        for row in range(8):
            ctab[pl.ds(8 * half + row, 16, stride=16), :] = cots[half, row].astype(F32)

    pool_copies = []
    for m in range(4):
        if m % 2 == 0:
            pl.when(r.far_exists)(far_halos[m // 2].wait_recv)
            lay_plane(xin, xk, far, (m, m + 1))
            both = pl.ds(128 * m, 256)
            pre[both] = pre[both] + jnp.dot(xk[far, both], wf[far], preferred_element_type=F32)
        span = pl.ds(128 * m, 128)
        v = pre[span]
        s = 0.5 * jnp.tanh(0.5 * v) + 0.5
        z = v * s
        e = jnp.exp(z)
        act[span] = z
        pe[span] = e * (s * (1.0 + (v - z)))
        n = e * z
        sum_e[span] = e[:, :128] + e[:, 128:]
        sum_n[span] = n[:, :128] + n[:, 128:]
        half = pl.ds(64 * m, 64)
        even = pl.ds(128 * m, 64, stride=2)
        odd = pl.ds(128 * m + 1, 64, stride=2)
        sums[m, 0] = sum_e[even, :] + sum_e[odd, :]
        sums[m, 1] = sum_n[even, :] + sum_n[odd, :]
        cp = remote(sums.at[m], psums.at[m], pool_send.at[m], pool_recv.at[m], r.partner)
        cp.start()
        pool_copies.append(cp)
    flip_plane(xk, xt, far)
    row = lax.rem(lax.broadcasted_iota(jnp.int32, (128, 256), 0), side)
    bias_part = jnp.zeros((1, 256), F32)
    for m in range(4):
        pool_copies[m].wait_recv()
        den = sums[m, 0] + psums[m, 0]
        value = (sums[m, 1] + psums[m, 1]) / den
        half = pl.ds(64 * m, 64)
        pvt[half] = value
        cb = ctab[half] / den
        ca = cb * (1.0 - value)
        even = pl.ds(128 * m, 64, stride=2)
        odd = pl.ds(128 * m + 1, 64, stride=2)
        fa[even, :] = ca
        fa[odd, :] = ca
        fb[even, :] = cb
        fb[odd, :] = cb
        span = pl.ds(128 * m, 128)
        wide_a = jnp.concatenate([fa[span], fa[span]], axis=1)
        wide_b = jnp.concatenate([fb[span], fb[span]], axis=1)
        g = (pe[span] * (wide_a + wide_b * act[span])).astype(BF16)
        gs[1, side + 128 * m : side + 128 * m + 128, :] = g
        g = g.astype(F32)
        bias_part = bias_part + jnp.sum(g, axis=0, keepdims=True)
        after = jnp.where(row == side - 1, 0.0, pltpu.roll(g, 127, 0))
        before = jnp.where(row == 0, 0.0, pltpu.roll(g, 1, 0))
        gs[0, side + 128 * m : side + 128 * m + 128, :] = after.astype(BF16)
        gs[2, side + 128 * m : side + 128 * m + 128, :] = before.astype(BF16)

    half = pl.ds(pl.multiple_of(core * 32, 32), 32)
    far_half = pl.ds(pl.multiple_of(32 - core * 32, 32), 32)
    core_copies = []
    part[27] = jnp.zeros((64, 128), F32)
    part[27, 0:1, :] = bias_part[:, :128] + bias_part[:, 128:]
    rs_copies = []

    def pass_on(g):
        count = 3 if g < 8 else 4
        span = pl.ds(3 * g, count)
        core_copies[g].wait_recv()
        rows[span] = (part[span, half, :] + theirs[span].astype(F32)).astype(BF16)
        for piece in range(3 * g, 3 * g + count):
            who, slot = r.owner_of(piece)
            is_me = jnp.logical_and(r.owner, r.piece == piece)
            taps_of = rows.at[pl.ds(piece, 1)]
            cp = remote(taps_of, rs.at[slot], rs_send.at[piece], rs_recv, who)
            unless(is_me, cp.start, local(taps_of, rs.at[r.slot], rs_recv).start)
            rs_copies.append((is_me, cp))

    turned = xt[...].reshape(768, cells)
    for b in range(3):
        stack = jnp.dot(turned, gs[b, side : side + cells, :], preferred_element_type=F32)
        for a in range(3):
            g = b * 3 + a
            block = stack[256 * a : 256 * a + 256]
            part[3 * g] = block[192:256, :128] + block[0:64, 128:]
            part[3 * g + 1] = block[0:64, :128] + block[64:128, 128:]
            part[3 * g + 2] = block[64:128, :128] + block[128:192, 128:]
            span = pl.ds(3 * g, 3 if g < 8 else 4)
            mine[span] = part[span, far_half, :].astype(BF16)
            cp = remote(mine.at[span], theirs.at[span], core_send.at[g], core_recv.at[g], r.partner)
            cp.start()
            core_copies.append(cp)
        if b:
            for g in range(3 * b - 3, 3 * b):
                pass_on(g)
    for g in range(6, 9):
        pass_on(g)
    for m in range(4):
        at = 128 * m
        total = jnp.zeros((128, 384), F32)
        for b in range(3):
            wide = jnp.concatenate(
                [
                    gs[b, at : at + 128, 128:256],
                    gs[b, at + 32 : at + 160, :],
                    gs[b, at + 64 : at + 192, 0:128],
                ],
                axis=1,
            )
            total = total + lax.dot_general(
                wide, wb[b], (((1,), (1,)), ((), ())), preferred_element_type=F32
            )
        for a in range(3):
            bt[a, at : at + 128, :] = total[:, 128 * a : 128 * a + 128].astype(BF16)
    bt_far = remote(bt.at[far], in_bt.at[far], bt_send.at[0], bt_recv.at[0], r.far)

    @pl.when(r.far_exists)
    def _():
        bt_far.start()

    bt_near = remote(bt.at[near], in_bt.at[near], bt_send.at[1], bt_recv.at[1], r.partner)
    bt_near.start()
    for row in range(8):
        pooled_out[row] = pvt[pl.ds(8 * core + row, 16, stride=16), :].astype(BF16)

    outs = [local(pooled_out, pooled_ref.at[0], out_sem.at[0])]
    outs[0].start()
    @pl.when(r.owner)
    def _():
        local(rs, rs, rs_recv).wait()
        total = rs[0].astype(F32)
        for i in range(1, 32):
            total = total + rs[i].astype(F32)
        ring_src[...] = total.astype(BF16)
        for i in range(7):
            cp = remote(ring_src, ring.at[r.ring_at], ring_send.at[i], ring_recv, r.ring_peer(i))
            cp.start()
        local(ring_src, ring.at[r.ring_at], ring_recv).start()
        local(ring, ring, ring_recv).wait()
        total = ring[0].astype(F32)
        for i in range(1, 8):
            total = total + ring[i].astype(F32)
        final[...] = total.astype(BF16)
        place_of = gath.at[core, pl.ds(per_piece * r.piece, per_piece)]
        for i in range(31):
            cp = remote(final, place_of, ag_send.at[i], ag_recv.at[lax.div(r.piece, 7)], r.plane_peer(i))
            cp.start()
        local(final, place_of, ag_recv.at[lax.div(r.piece, 7)]).start()

    bt_near.wait()

    @pl.when(r.far_exists)
    def _():
        bt_far.wait()

    for q in range(pairs):
        span = pl.ds(side * q, side)
        summed = in_bt[0, span].astype(F32) + bt[1, span].astype(F32) + in_bt[2, span].astype(F32)
        input_grad_out[:, 128 * q : 128 * q + 128] = summed.astype(BF16)
    outs.append(local(input_grad_out, input_grad_ref.at[0, 0], out_sem.at[1]))
    outs[1].start()

    fw_copies = []
    for kind in range(4):
        span = gath.at[core, pl.ds(7 * kind, 7)]
        local(span, span, ag_recv.at[kind]).wait()
        cp = remote(span, span, fw_send.at[kind], fw_recv.at[kind], r.partner)
        cp.start()
        outs.append(local(span, sum_ref.at[core, pl.ds(7 * kind, 7)], out_sem.at[2 + kind]))
        outs[-1].start()
        fw_copies.append(cp)
    for kind in range(4):
        fw_copies[kind].wait()
        span = pl.ds(7 * kind, 7)
        outs.append(local(gath.at[1 - core, span], sum_ref.at[1 - core, span], out_sem.at[6 + kind]))
        outs[-1].start()
    for cp in core_copies + pool_copies + [near_halo, cot_copy]:
        cp.wait_send()

    @pl.when(r.far_exists)
    def _():
        for cp in far_halos:
            cp.wait_send()

    for is_me, cp in rs_copies:
        unless(is_me, cp.wait_send)

    @pl.when(r.owner)
    def _():
        for i in range(7):
            local(ring_src, ring_src, ring_send.at[i]).wait()
        for i in range(31):
            local(final, final, ag_send.at[i]).wait()

    for cp in outs:
        cp.wait()


def hand_over(
    pooled, input_grad, total, pooled_ref, input_grad_ref, weight_ref, bias_ref, t, g, p, w, bias, get, put
):
    groups = (pl.ds(0, 9), pl.ds(9, 9), pl.ds(18, 10))
    reads = [local(total.at[:, span], t.at[:, span], get.at[i]) for i, span in enumerate(groups)]
    reads += [local(input_grad, g, get.at[3]), local(pooled, p, get.at[4])]
    for cp in reads:
        cp.start()
    writes = []
    for b in range(3):
        reads[b].wait()
        for a in range(3):
            first, at = 9 * b + 3 * a, 9 * a + 3 * b
            for h in range(2):
                w[at : at + 3, 32 * h : 32 * h + 32, :] = t[h, first : first + 3].astype(F32) * (1.0 / loss_scale)
            writes.append(local(w.at[pl.ds(at, 3)], weight_ref.at[pl.ds(at, 3)], put.at[3 * b + a]))
            writes[-1].start()
    bias[...] = t[0, taps, 0, :].astype(F32) * (1.0 / loss_scale)
    writes.append(local(bias, bias_ref, put.at[9]))
    writes[-1].start()
    reads[3].wait()
    writes.append(local(g, input_grad_ref, put.at[10]))
    writes[-1].start()
    reads[4].wait()
    writes.append(local(p, pooled_ref, put.at[11]))
    writes[-1].start()
    for cp in writes:
        cp.wait()


def block(volume, weight, conv_bias, cotangent):
    dma = pltpu.SemaphoreType.DMA
    vmem = pltpu.VMEM
    anywhere = pl.BlockSpec(memory_space=pltpu.HBM)
    shapes = (
        jax.ShapeDtypeStruct(cotangent.shape, BF16),
        jax.ShapeDtypeStruct(volume.shape, BF16),
        jax.ShapeDtypeStruct((taps, 64, 128), F32),
        jax.ShapeDtypeStruct(conv_bias.shape, F32),
    )
    sums = jax.ShapeDtypeStruct((2, blocks, 32, 128), BF16)
    results = pl.pallas_call(
        block_kernel,
        out_shape=shapes[:2] + (sums,),
        in_specs=[anywhere] * 4,
        out_specs=(anywhere,) * 3,
        scratch_shapes=[
            vmem((3, side, 2304), BF16),
            vmem((3, 3, 3, 64, 128), BF16),
            vmem((128,), F32),
            vmem((2, 8, 16, 128), BF16),
            vmem((3, 768, 256), BF16),
            vmem((3, 384, 512), BF16),
            vmem((3, cells, 768), BF16),
            vmem((3, 256, cells), BF16),
            vmem((cells, 256), F32),
            vmem((cells, 256), F32),
            vmem((cells, 256), F32),
            vmem((cells, 128), F32),
            vmem((cells, 128), F32),
            vmem((4, 2, 64, 128), F32),
            vmem((4, 2, 64, 128), F32),
            vmem((256, 128), F32),
            vmem((256, 128), F32),
            vmem((cells, 128), F32),
            vmem((cells, 128), F32),
            vmem((3, cells + 2 * side, 256), BF16),
            vmem((blocks, 64, 128), F32),
            vmem((3, cells, 128), BF16),
            vmem((3, cells, 128), BF16),
            vmem((blocks, 32, 128), BF16),
            vmem((blocks, 32, 128), BF16),
            vmem((blocks, 32, 128), BF16),
            vmem((32, per_piece, 32, 128), BF16),
            vmem((per_piece, 32, 128), BF16),
            vmem((8, per_piece, 32, 128), BF16),
            vmem((per_piece, 32, 128), BF16),
            vmem((2, blocks, 32, 128), BF16),
            vmem((8, 16, 128), BF16),
            vmem((side, 2048), BF16),
            dma((4,)), dma((3,)), dma((3,)), dma, dma, dma((4,)), dma((4,)), dma((2,)), dma((2,)),
            dma((9,)), dma((9,)), dma((pieces,)), dma, dma((8,)), dma, dma((32,)), dma((4,)), dma((4,)), dma((4,)), dma((10,)),
        ],
        compiler_params=pltpu.CompilerParams(
            collective_id=0, has_side_effects=True, vmem_limit_bytes=62 * 2**20
        ),
        name="conv_block",
    )(volume, weight, conv_bias, cotangent)
    pooled, input_grad, weight_grad, bias_grad = pl.pallas_call(
        hand_over,
        out_shape=shapes,
        in_specs=[anywhere] * 3,
        out_specs=(anywhere,) * 4,
        scratch_shapes=[vmem(v.shape, v.dtype) for v in (sums, shapes[1], shapes[0], shapes[2], shapes[3])]
        + [dma((5,)), dma((12,))],
        compiler_params=pltpu.CompilerParams(vmem_limit_bytes=62 * 2**20),
        name="hand_over",
    )(*results)
    return pooled, input_grad, weight_grad.reshape(weight.shape), bias_grad


def solution(mesh):
    placed = (P("sample", "space", None, None), P(), P(), P("sample", "space", None, None))
    return jax.shard_map(
        block,
        mesh=mesh,
        in_specs=placed,
        out_specs=(P("sample", "space", None, None), P("sample", "space", None, None), P(), P()),
        check_vma=False,
    )
```

```python
import jax
import jax.numpy as jnp
from jax import lax
from jax.experimental import pallas as pl
from jax.experimental.pallas import tpu as pltpu
from jax.sharding import PartitionSpec as P

MESH = pl.DeviceIdType.MESH
BF16 = jnp.bfloat16
F32 = jnp.float32
taps = 27
blocks = 28
per_piece = 1
pieces = blocks // per_piece
per_kind = pieces // 2
side = 32
pairs = 16
cells = 512
loss_scale = 256.0
spots = tuple((x, row) for row in (4, 3, 5, 2, 6, 1, 0) for x in (1, 0))


def place():
    space = lax.axis_index("space")
    sample = lax.axis_index("sample")
    core = lax.rem(space, 2)
    z_lo = lax.rem(lax.div(space, 2), 4)
    y = lax.div(space, 8)
    z = lax.div(sample, 4) * 4 + z_lo
    x = lax.rem(sample, 4)
    return x, y, z, core


def ident(x, y, z, core):
    return ((y * 4 + lax.rem(z, 4)) * 2 + core, lax.div(z, 4) * 4 + x)


class Reduce:
    def __init__(self):
        self.x, self.y, self.z, self.core = place()
        x, y, z = self.x, self.y, self.z
        self.kind_a = x < 2
        self.ring_at = jnp.where(self.kind_a, z, y)
        self.row_at = jnp.where(self.kind_a, y, z)
        self.kind = jnp.where(self.kind_a, 0, 1)
        side_x = jnp.where(self.kind_a, x, 3 - x)
        self.owner = False
        self.piece = 0
        for i, (sx, row) in enumerate(spots):
            here = jnp.logical_and(side_x == sx, self.row_at == row)
            self.owner = jnp.logical_or(self.owner, here)
            self.piece = self.piece + jnp.where(here, i, 0)
        self.piece = 2 * self.piece + self.kind
        self.slot = x * 8 + self.row_at
        self.partner = ident(x, y, z, 1 - self.core)
        plane = lax.axis_index("space")
        far_plane = plane + 2 * self.core - 1
        self.far_exists = jnp.logical_and(far_plane >= 0, far_plane < lax.axis_size("space"))
        self.far = (jnp.clip(far_plane, 0, lax.axis_size("space") - 1), lax.axis_index("sample"))
        self.near_tap = 2 - 2 * self.core
        self.far_tap = 2 * self.core

    def plane_peer(self, i):
        at = i + jnp.where(i >= self.row_at * 4 + self.x, 1, 0)
        row = lax.div(at, 4)
        y = jnp.where(self.kind_a, row, self.y)
        z = jnp.where(self.kind_a, self.z, row)
        return ident(lax.rem(at, 4), y, z, self.core)

    def ring_peer(self, i):
        at = i + jnp.where(i >= self.ring_at, 1, 0)
        y = jnp.where(self.kind_a, self.y, at)
        z = jnp.where(self.kind_a, at, self.z)
        return ident(self.x, y, z, self.core)

    def owner_of(self, piece):
        i, kind = divmod(piece, 2)
        x, row = spots[i]
        if kind == 0:
            return ident(x, row, self.z, self.core), self.x * 8 + self.y
        return ident(3 - x, self.y, row, self.core), self.x * 8 + self.z


def unless(me, action, otherwise=None):
    pl.when(jnp.logical_not(me))(action)
    if otherwise is not None:
        pl.when(me)(otherwise)


def signal(sem, who):
    pl.semaphore_signal(sem, inc=1, device_id=who, device_id_type=MESH)


def remote(src, dst, send, recv, who):
    return pltpu.make_async_remote_copy(
        src_ref=src, dst_ref=dst, send_sem=send, recv_sem=recv, device_id=who, device_id_type=MESH
    )


def local(src, dst, sem):
    return pltpu.make_async_copy(src, dst, sem)


def lay_weights(wraw, wf, wb):
    none = jnp.zeros((64, 128), BF16)
    for a in range(3):
        for b in range(3):
            t0, t1, t2 = (wraw[a, b, c] for c in range(3))
            for cell, column in enumerate(((t1, t2, none, t0), (t0, t1, t2, none))):
                for k, block in enumerate(column):
                    wf[a, 256 * b + 64 * k : 256 * b + 64 * k + 64, 128 * cell : 128 * cell + 128] = block
            for cell, row in enumerate(((t2, t1, t0, none), (none, t2, t1, t0))):
                at = (2 * a + cell) * 64
                for j, block in enumerate(row):
                    wb[b, at : at + 64, 128 * j : 128 * j + 128] = block


def lay_plane(xin, xk, p, chunks=range(4)):
    width = 512
    row = lax.broadcasted_iota(jnp.int32, (side, width), 0)
    low = lax.rem(lax.broadcasted_iota(jnp.int32, (side, width), 1), 128) < 64
    first, last = row == 0, row == side - 1
    for chunk in chunks:
        at = width * chunk
        left = xin[p, :, at : at + width].astype(F32)
        here = xin[p, :, at + 128 : at + 128 + width].astype(F32)
        right = xin[p, :, at + 256 : at + 256 + width].astype(F32)
        beside = jnp.where(low, right, left)
        for k, value in enumerate((here, beside)):
            up = jnp.where(first, 0.0, pltpu.roll(value, 1, 0))
            down = jnp.where(last, 0.0, pltpu.roll(value, side - 1, 0))
            for b, shifted in enumerate((up, value, down)):
                shifted = shifted.astype(BF16)
                for i in range(4):
                    q = 4 * chunk + i
                    lane = 256 * b + 128 * k
                    xk[p, side * q : side * q + side, lane : lane + 128] = shifted[:, 128 * i : 128 * i + 128]


def flip_plane(xk, xt, p):
    xt[p] = xk[p, :, 256:512].T


def block_kernel(
    volume_ref, weight_ref, bias_hbm, cot_ref,
    pooled_ref, input_grad_ref, sum_ref,
    xin, wraw, bias_ref, cots, wf, wb, xk, xt, pre, act, pe, sum_e, sum_n, sums, psums, ctab, pvt, fa, fb, gs, part, bt, in_bt,
    mine, theirs, rows, rs, ring_src, ring, final,
    gath, pooled_out, input_grad_out,
    load_sem, halo_send, halo_recv, cot_send, cot_recv, pool_send, pool_recv, bt_send, bt_recv,
    core_send, core_recv, rs_send, rs_recv, ring_send, ring_recv, ag_send, ag_recv, fw_send, fw_recv, out_sem,
):
    r = Reduce()
    core = r.core
    near, far = r.near_tap, r.far_tap
    body_lanes = pl.ds(128, 2048)
    bar = pltpu.get_barrier_semaphore()

    @pl.when(r.far_exists)
    def _():
        signal(bar, r.far)

    signal(bar, r.partner)
    loads = [
        local(volume_ref.at[0, 0], xin.at[1, :, body_lanes], load_sem.at[0]),
        local(cot_ref.at[0], cots.at[core], load_sem.at[1]),
        local(weight_ref, wraw, load_sem.at[2]),
        local(bias_hbm, bias_ref, load_sem.at[3]),
    ]
    for cp in loads:
        cp.start()

    @pl.when(r.owner)
    def _():
        for i in reversed(range(31)):
            signal(bar, r.plane_peer(i))
        for i in range(7):
            signal(bar, r.ring_peer(i))

    for p in range(3):
        xin[p, :, 0:128] = jnp.zeros((side, 128), BF16)
        xin[p, :, 2176:2304] = jnp.zeros((side, 128), BF16)

    @pl.when(jnp.logical_not(r.far_exists))
    def _():
        xin[far] = jnp.zeros((side, 2304), BF16)
        in_bt[2 - far] = jnp.zeros((cells, 128), BF16)

    for cp in loads:
        cp.wait()
    own = jnp.where(r.owner, 1, 0)
    pl.semaphore_wait(bar, pieces + 1 + 6 * own + jnp.where(r.far_exists, 1, 0))

    own_plane = xin.at[1, :, body_lanes]
    far_halos = []
    for i, lanes in enumerate((pl.ds(128, 9 * 128), pl.ds(10 * 128, 7 * 128))):
        src = xin.at[1, :, lanes]
        far_halos.append(remote(src, xin.at[2 - far, :, lanes], halo_send.at[2 * i], halo_recv.at[2 * i], r.far))

    @pl.when(r.far_exists)
    def _():
        for cp in far_halos:
            cp.start()

    near_halo = remote(own_plane, xin.at[2 - near, :, body_lanes], halo_send.at[1], halo_recv.at[1], r.partner)
    near_halo.start()
    cot_copy = remote(cots.at[core], cots.at[core], cot_send, cot_recv, r.partner)
    cot_copy.start()

    lay_weights(wraw, wf, wb)
    for b in range(3):
        gs[b, 0:side, :] = jnp.zeros((side, 256), BF16)
        gs[b, side + cells : 2 * side + cells, :] = jnp.zeros((side, 256), BF16)
    lay_plane(xin, xk, 1)
    flip_plane(xk, xt, 1)
    near_halo.wait_recv()
    lay_plane(xin, xk, near)
    bias = bias_ref[...].reshape(1, 128)
    bias = jnp.concatenate([bias, bias], axis=1)
    for m in range(2):
        span = pl.ds(256 * m, 256)
        pre[span] = (
            bias
            + jnp.dot(xk[1, span], wf[1], preferred_element_type=F32)
            + jnp.dot(xk[near, span], wf[near], preferred_element_type=F32)
        )
    flip_plane(xk, xt, near)
    cot_copy.wait_recv()
    for half in range(2):
        for row in range(8):
            ctab[pl.ds(8 * half + row, 16, stride=16), :] = cots[half, row].astype(F32)

    pool_copies = []
    for m in range(4):
        if m % 2 == 0:
            pl.when(r.far_exists)(far_halos[m // 2].wait_recv)
            lay_plane(xin, xk, far, (m, m + 1))
            both = pl.ds(128 * m, 256)
            pre[both] = pre[both] + jnp.dot(xk[far, both], wf[far], preferred_element_type=F32)
        span = pl.ds(128 * m, 128)
        v = pre[span]
        s = 0.5 * jnp.tanh(0.5 * v) + 0.5
        z = v * s
        e = jnp.exp(z)
        act[span] = z
        pe[span] = e * (s * (1.0 + (v - z)))
        n = e * z
        sum_e[span] = e[:, :128] + e[:, 128:]
        sum_n[span] = n[:, :128] + n[:, 128:]
        half = pl.ds(64 * m, 64)
        even = pl.ds(128 * m, 64, stride=2)
        odd = pl.ds(128 * m + 1, 64, stride=2)
        sums[m, 0] = sum_e[even, :] + sum_e[odd, :]
        sums[m, 1] = sum_n[even, :] + sum_n[odd, :]
        cp = remote(sums.at[m], psums.at[m], pool_send.at[m], pool_recv.at[m], r.partner)
        cp.start()
        pool_copies.append(cp)
    flip_plane(xk, xt, far)
    row = lax.rem(lax.broadcasted_iota(jnp.int32, (128, 256), 0), side)
    bias_part = jnp.zeros((1, 256), F32)
    for m in range(4):
        pool_copies[m].wait_recv()
        den = sums[m, 0] + psums[m, 0]
        value = (sums[m, 1] + psums[m, 1]) / den
        half = pl.ds(64 * m, 64)
        pvt[half] = value
        cb = ctab[half] / den
        ca = cb * (1.0 - value)
        even = pl.ds(128 * m, 64, stride=2)
        odd = pl.ds(128 * m + 1, 64, stride=2)
        fa[even, :] = ca
        fa[odd, :] = ca
        fb[even, :] = cb
        fb[odd, :] = cb
        span = pl.ds(128 * m, 128)
        wide_a = jnp.concatenate([fa[span], fa[span]], axis=1)
        wide_b = jnp.concatenate([fb[span], fb[span]], axis=1)
        g = (pe[span] * (wide_a + wide_b * act[span])).astype(BF16)
        gs[1, side + 128 * m : side + 128 * m + 128, :] = g
        g = g.astype(F32)
        bias_part = bias_part + jnp.sum(g, axis=0, keepdims=True)
        after = jnp.where(row == side - 1, 0.0, pltpu.roll(g, 127, 0))
        before = jnp.where(row == 0, 0.0, pltpu.roll(g, 1, 0))
        gs[0, side + 128 * m : side + 128 * m + 128, :] = after.astype(BF16)
        gs[2, side + 128 * m : side + 128 * m + 128, :] = before.astype(BF16)

    half = pl.ds(pl.multiple_of(core * 32, 32), 32)
    far_half = pl.ds(pl.multiple_of(32 - core * 32, 32), 32)
    core_copies = []
    part[27] = jnp.zeros((64, 128), F32)
    part[27, 0:1, :] = bias_part[:, :128] + bias_part[:, 128:]
    rs_copies = []

    def pass_on(g):
        count = 3 if g < 8 else 4
        span = pl.ds(3 * g, count)
        core_copies[g].wait_recv()
        rows[span] = (part[span, half, :] + theirs[span].astype(F32)).astype(BF16)
        for piece in range(3 * g, 3 * g + count):
            who, slot = r.owner_of(piece)
            is_me = jnp.logical_and(r.owner, r.piece == piece)
            taps_of = rows.at[pl.ds(piece, 1)]
            cp = remote(taps_of, rs.at[slot], rs_send.at[piece], rs_recv, who)
            unless(is_me, cp.start, local(taps_of, rs.at[r.slot], rs_recv).start)
            rs_copies.append((is_me, cp))

    turned = xt[...].reshape(768, cells)
    for b in range(3):
        stack = jnp.dot(turned, gs[b, side : side + cells, :], preferred_element_type=F32)
        for a in range(3):
            g = b * 3 + a
            block = stack[256 * a : 256 * a + 256]
            part[3 * g] = block[192:256, :128] + block[0:64, 128:]
            part[3 * g + 1] = block[0:64, :128] + block[64:128, 128:]
            part[3 * g + 2] = block[64:128, :128] + block[128:192, 128:]
            span = pl.ds(3 * g, 3 if g < 8 else 4)
            mine[span] = part[span, far_half, :].astype(BF16)
            cp = remote(mine.at[span], theirs.at[span], core_send.at[g], core_recv.at[g], r.partner)
            cp.start()
            core_copies.append(cp)
        if b:
            for g in range(3 * b - 3, 3 * b):
                pass_on(g)
    for g in range(6, 9):
        pass_on(g)
    for m in range(4):
        at = 128 * m
        total = jnp.zeros((128, 384), F32)
        for b in range(3):
            wide = jnp.concatenate(
                [
                    gs[b, at : at + 128, 128:256],
                    gs[b, at + 32 : at + 160, :],
                    gs[b, at + 64 : at + 192, 0:128],
                ],
                axis=1,
            )
            total = total + lax.dot_general(
                wide, wb[b], (((1,), (1,)), ((), ())), preferred_element_type=F32
            )
        for a in range(3):
            bt[a, at : at + 128, :] = total[:, 128 * a : 128 * a + 128].astype(BF16)
    bt_far = remote(bt.at[far], in_bt.at[far], bt_send.at[0], bt_recv.at[0], r.far)

    @pl.when(r.far_exists)
    def _():
        bt_far.start()

    bt_near = remote(bt.at[near], in_bt.at[near], bt_send.at[1], bt_recv.at[1], r.partner)
    bt_near.start()
    for row in range(8):
        pooled_out[row] = pvt[pl.ds(8 * core + row, 16, stride=16), :].astype(BF16)

    outs = [local(pooled_out, pooled_ref.at[0], out_sem.at[0])]
    outs[0].start()
    @pl.when(r.owner)
    def _():
        local(rs, rs, rs_recv).wait()
        total = rs[0].astype(F32)
        for i in range(1, 32):
            total = total + rs[i].astype(F32)
        ring_src[...] = total.astype(BF16)
        for i in range(7):
            cp = remote(ring_src, ring.at[r.ring_at], ring_send.at[i], ring_recv, r.ring_peer(i))
            cp.start()
        local(ring_src, ring.at[r.ring_at], ring_recv).start()
        local(ring, ring, ring_recv).wait()
        total = ring[0].astype(F32)
        for i in range(1, 8):
            total = total + ring[i].astype(F32)
        final[...] = total.astype(BF16)
        place_of = gath.at[pl.ds(per_piece * r.piece, per_piece)]
        for i in range(31):
            cp = remote(final, place_of, ag_send.at[i], ag_recv.at[lax.div(r.piece, 7)], r.plane_peer(i))
            cp.start()
        local(final, place_of, ag_recv.at[lax.div(r.piece, 7)]).start()

    bt_near.wait()

    @pl.when(r.far_exists)
    def _():
        bt_far.wait()

    for q in range(pairs):
        span = pl.ds(side * q, side)
        summed = in_bt[0, span].astype(F32) + bt[1, span].astype(F32) + in_bt[2, span].astype(F32)
        input_grad_out[:, 128 * q : 128 * q + 128] = summed.astype(BF16)
    outs.append(local(input_grad_out, input_grad_ref.at[0, 0], out_sem.at[1]))
    outs[1].start()

    fw_copies = []
    for kind in range(4):
        span = gath.at[pl.ds(7 * kind, 7)]
        local(span, span, ag_recv.at[kind]).wait()
        cp = remote(span, sum_ref.at[core, pl.ds(7 * kind, 7)], fw_send.at[kind], fw_recv.at[kind], r.partner)
        cp.start()
        outs.append(local(span, sum_ref.at[core, pl.ds(7 * kind, 7)], out_sem.at[2 + kind]))
        outs[-1].start()
        fw_copies.append(cp)
    for kind in range(4):
        fw_copies[kind].wait()
    for cp in core_copies + pool_copies + [near_halo, cot_copy]:
        cp.wait_send()

    @pl.when(r.far_exists)
    def _():
        for cp in far_halos:
            cp.wait_send()

    for is_me, cp in rs_copies:
        unless(is_me, cp.wait_send)

    @pl.when(r.owner)
    def _():
        for i in range(7):
            local(ring_src, ring_src, ring_send.at[i]).wait()
        for i in range(31):
            local(final, final, ag_send.at[i]).wait()

    for cp in outs:
        cp.wait()


def hand_over(
    pooled, input_grad, total, pooled_ref, input_grad_ref, weight_ref, bias_ref, t, g, p, w, bias, get, put
):
    groups = (pl.ds(0, 9), pl.ds(9, 9), pl.ds(18, 10))
    reads = [local(total.at[:, span], t.at[:, span], get.at[i]) for i, span in enumerate(groups)]
    reads += [local(input_grad, g, get.at[3]), local(pooled, p, get.at[4])]
    for cp in reads:
        cp.start()
    writes = []
    for b in range(3):
        reads[b].wait()
        for a in range(3):
            first, at = 9 * b + 3 * a, 9 * a + 3 * b
            for h in range(2):
                w[at : at + 3, 32 * h : 32 * h + 32, :] = t[h, first : first + 3].astype(F32) * (1.0 / loss_scale)
            writes.append(local(w.at[pl.ds(at, 3)], weight_ref.at[pl.ds(at, 3)], put.at[3 * b + a]))
            writes[-1].start()
    bias[...] = t[0, taps, 0, :].astype(F32) * (1.0 / loss_scale)
    writes.append(local(bias, bias_ref, put.at[9]))
    writes[-1].start()
    reads[3].wait()
    writes.append(local(g, input_grad_ref, put.at[10]))
    writes[-1].start()
    reads[4].wait()
    writes.append(local(p, pooled_ref, put.at[11]))
    writes[-1].start()
    for cp in writes:
        cp.wait()


def block(volume, weight, conv_bias, cotangent):
    dma = pltpu.SemaphoreType.DMA
    vmem = pltpu.VMEM
    anywhere = pl.BlockSpec(memory_space=pltpu.HBM)
    shapes = (
        jax.ShapeDtypeStruct(cotangent.shape, BF16),
        jax.ShapeDtypeStruct(volume.shape, BF16),
        jax.ShapeDtypeStruct((taps, 64, 128), F32),
        jax.ShapeDtypeStruct(conv_bias.shape, F32),
    )
    sums = jax.ShapeDtypeStruct((2, blocks, 32, 128), BF16)
    results = pl.pallas_call(
        block_kernel,
        out_shape=shapes[:2] + (sums,),
        in_specs=[anywhere] * 4,
        out_specs=(anywhere,) * 3,
        scratch_shapes=[
            vmem((3, side, 2304), BF16),
            vmem((3, 3, 3, 64, 128), BF16),
            vmem((128,), F32),
            vmem((2, 8, 16, 128), BF16),
            vmem((3, 768, 256), BF16),
            vmem((3, 384, 512), BF16),
            vmem((3, cells, 768), BF16),
            vmem((3, 256, cells), BF16),
            vmem((cells, 256), F32),
            vmem((cells, 256), F32),
            vmem((cells, 256), F32),
            vmem((cells, 128), F32),
            vmem((cells, 128), F32),
            vmem((4, 2, 64, 128), F32),
            vmem((4, 2, 64, 128), F32),
            vmem((256, 128), F32),
            vmem((256, 128), F32),
            vmem((cells, 128), F32),
            vmem((cells, 128), F32),
            vmem((3, cells + 2 * side, 256), BF16),
            vmem((blocks, 64, 128), F32),
            vmem((3, cells, 128), BF16),
            vmem((3, cells, 128), BF16),
            vmem((blocks, 32, 128), BF16),
            vmem((blocks, 32, 128), BF16),
            vmem((blocks, 32, 128), BF16),
            vmem((32, per_piece, 32, 128), BF16),
            vmem((per_piece, 32, 128), BF16),
            vmem((8, per_piece, 32, 128), BF16),
            vmem((per_piece, 32, 128), BF16),
            vmem((blocks, 32, 128), BF16),
            vmem((8, 16, 128), BF16),
            vmem((side, 2048), BF16),
            dma((4,)), dma((3,)), dma((3,)), dma, dma, dma((4,)), dma((4,)), dma((2,)), dma((2,)),
            dma((9,)), dma((9,)), dma((pieces,)), dma, dma((8,)), dma, dma((32,)), dma((4,)), dma((4,)), dma((4,)), dma((6,)),
        ],
        compiler_params=pltpu.CompilerParams(
            collective_id=0, has_side_effects=True, vmem_limit_bytes=62 * 2**20
        ),
        name="conv_block",
    )(volume, weight, conv_bias, cotangent)
    pooled, input_grad, weight_grad, bias_grad = pl.pallas_call(
        hand_over,
        out_shape=shapes,
        in_specs=[anywhere] * 3,
        out_specs=(anywhere,) * 4,
        scratch_shapes=[vmem(v.shape, v.dtype) for v in (sums, shapes[1], shapes[0], shapes[2], shapes[3])]
        + [dma((5,)), dma((12,))],
        compiler_params=pltpu.CompilerParams(vmem_limit_bytes=62 * 2**20),
        name="hand_over",
    )(*results)
    return pooled, input_grad, weight_grad.reshape(weight.shape), bias_grad


def solution(mesh):
    placed = (P("sample", "space", None, None), P(), P(), P("sample", "space", None, None))
    return jax.shard_map(
        block,
        mesh=mesh,
        in_specs=placed,
        out_specs=(P("sample", "space", None, None), P("sample", "space", None, None), P(), P()),
        check_vma=False,
    )
```

```python
import jax
import jax.numpy as jnp
from jax import lax
from jax.experimental import pallas as pl
from jax.experimental.pallas import tpu as pltpu
from jax.sharding import PartitionSpec as P

MESH = pl.DeviceIdType.MESH
BF16 = jnp.bfloat16
F32 = jnp.float32
taps = 27
blocks = 28
per_piece = 1
pieces = blocks // per_piece
per_kind = pieces // 2
side = 32
pairs = 16
cells = 512
loss_scale = 256.0
spots = tuple((x, row) for row in (4, 3, 5, 2, 6, 1, 0) for x in (1, 0))


def place():
    space = lax.axis_index("space")
    sample = lax.axis_index("sample")
    core = lax.rem(space, 2)
    z_lo = lax.rem(lax.div(space, 2), 4)
    y = lax.div(space, 8)
    z = lax.div(sample, 4) * 4 + z_lo
    x = lax.rem(sample, 4)
    return x, y, z, core


def ident(x, y, z, core):
    return ((y * 4 + lax.rem(z, 4)) * 2 + core, lax.div(z, 4) * 4 + x)


class Reduce:
    def __init__(self):
        self.x, self.y, self.z, self.core = place()
        x, y, z = self.x, self.y, self.z
        self.kind_a = x < 2
        self.ring_at = jnp.where(self.kind_a, z, y)
        self.row_at = jnp.where(self.kind_a, y, z)
        self.kind = jnp.where(self.kind_a, 0, 1)
        side_x = jnp.where(self.kind_a, x, 3 - x)
        self.owner = False
        self.piece = 0
        for i, (sx, row) in enumerate(spots):
            here = jnp.logical_and(side_x == sx, self.row_at == row)
            self.owner = jnp.logical_or(self.owner, here)
            self.piece = self.piece + jnp.where(here, i, 0)
        self.piece = 2 * self.piece + self.kind
        self.slot = x * 8 + self.row_at
        self.partner = ident(x, y, z, 1 - self.core)
        plane = lax.axis_index("space")
        far_plane = plane + 2 * self.core - 1
        self.far_exists = jnp.logical_and(far_plane >= 0, far_plane < lax.axis_size("space"))
        self.far = (jnp.clip(far_plane, 0, lax.axis_size("space") - 1), lax.axis_index("sample"))
        self.near_tap = 2 - 2 * self.core
        self.far_tap = 2 * self.core

    def plane_peer(self, i):
        at = i + jnp.where(i >= self.row_at * 4 + self.x, 1, 0)
        row = lax.div(at, 4)
        y = jnp.where(self.kind_a, row, self.y)
        z = jnp.where(self.kind_a, self.z, row)
        return ident(lax.rem(at, 4), y, z, self.core)

    def ring_peer(self, i):
        at = i + jnp.where(i >= self.ring_at, 1, 0)
        y = jnp.where(self.kind_a, self.y, at)
        z = jnp.where(self.kind_a, at, self.z)
        return ident(self.x, y, z, self.core)

    def owner_of(self, piece):
        i, kind = divmod(piece, 2)
        x, row = spots[i]
        if kind == 0:
            return ident(x, row, self.z, self.core), self.x * 8 + self.y
        return ident(3 - x, self.y, row, self.core), self.x * 8 + self.z


def unless(me, action, otherwise=None):
    pl.when(jnp.logical_not(me))(action)
    if otherwise is not None:
        pl.when(me)(otherwise)


def signal(sem, who):
    pl.semaphore_signal(sem, inc=1, device_id=who, device_id_type=MESH)


def remote(src, dst, send, recv, who):
    return pltpu.make_async_remote_copy(
        src_ref=src, dst_ref=dst, send_sem=send, recv_sem=recv, device_id=who, device_id_type=MESH
    )


def local(src, dst, sem):
    return pltpu.make_async_copy(src, dst, sem)


def lay_weights(wraw, wf, wb):
    none = jnp.zeros((64, 128), BF16)
    for a in range(3):
        for b in range(3):
            t0, t1, t2 = (wraw[a, b, c] for c in range(3))
            for cell, column in enumerate(((t1, t2, none, t0), (t0, t1, t2, none))):
                for k, block in enumerate(column):
                    wf[a, 256 * b + 64 * k : 256 * b + 64 * k + 64, 128 * cell : 128 * cell + 128] = block
            for cell, row in enumerate(((t2, t1, t0, none), (none, t2, t1, t0))):
                at = (2 * a + cell) * 64
                for j, block in enumerate(row):
                    wb[b, at : at + 64, 128 * j : 128 * j + 128] = block


def lay_plane(xin, xk, p, chunks=range(4)):
    width = 512
    row = lax.broadcasted_iota(jnp.int32, (side, width), 0)
    low = lax.rem(lax.broadcasted_iota(jnp.int32, (side, width), 1), 128) < 64
    first, last = row == 0, row == side - 1
    for chunk in chunks:
        at = width * chunk
        left = xin[p, :, at : at + width].astype(F32)
        here = xin[p, :, at + 128 : at + 128 + width].astype(F32)
        right = xin[p, :, at + 256 : at + 256 + width].astype(F32)
        beside = jnp.where(low, right, left)
        for k, value in enumerate((here, beside)):
            up = jnp.where(first, 0.0, pltpu.roll(value, 1, 0))
            down = jnp.where(last, 0.0, pltpu.roll(value, side - 1, 0))
            for b, shifted in enumerate((up, value, down)):
                shifted = shifted.astype(BF16)
                for i in range(4):
                    q = 4 * chunk + i
                    lane = 256 * b + 128 * k
                    xk[p, side * q : side * q + side, lane : lane + 128] = shifted[:, 128 * i : 128 * i + 128]


def flip_plane(xk, xt, p):
    xt[p] = xk[p, :, 256:512].T


def block_kernel(
    volume_ref, weight_ref, bias_hbm, cot_ref,
    pooled_ref, input_grad_ref, sum_ref,
    xin, wraw, bias_ref, cots, wf, wb, xk, xt, pre, act, pe, sum_e, sum_n, sums, psums, ctab, pvt, fa, fb, gs, part, bt, in_bt,
    mine, theirs, rows, rs, ring_src, ring, final,
    gath, pooled_out, input_grad_out,
    load_sem, halo_send, halo_recv, cot_send, cot_recv, pool_send, pool_recv, bt_send, bt_recv,
    core_send, core_recv, rs_send, rs_recv, ring_send, ring_recv, ag_send, ag_recv, fw_send, fw_recv, out_sem,
):
    r = Reduce()
    core = r.core
    near, far = r.near_tap, r.far_tap
    body_lanes = pl.ds(128, 2048)
    bar = pltpu.get_barrier_semaphore()

    @pl.when(r.far_exists)
    def _():
        signal(bar, r.far)

    signal(bar, r.partner)
    loads = [
        local(volume_ref.at[0, 0], xin.at[1, :, body_lanes], load_sem.at[0]),
        local(cot_ref.at[0], cots.at[core], load_sem.at[1]),
        local(weight_ref, wraw, load_sem.at[2]),
        local(bias_hbm, bias_ref, load_sem.at[3]),
    ]
    for cp in loads:
        cp.start()

    @pl.when(r.owner)
    def _():
        for i in reversed(range(31)):
            signal(bar, r.plane_peer(i))
        for i in range(7):
            signal(bar, r.ring_peer(i))

    for p in range(3):
        xin[p, :, 0:128] = jnp.zeros((side, 128), BF16)
        xin[p, :, 2176:2304] = jnp.zeros((side, 128), BF16)

    @pl.when(jnp.logical_not(r.far_exists))
    def _():
        xin[far] = jnp.zeros((side, 2304), BF16)
        in_bt[2 - far] = jnp.zeros((cells, 128), BF16)

    for cp in loads:
        cp.wait()
    own = jnp.where(r.owner, 1, 0)
    pl.semaphore_wait(bar, pieces + 1 + 6 * own + jnp.where(r.far_exists, 1, 0))

    own_plane = xin.at[1, :, body_lanes]
    far_halos = []
    for i, lanes in enumerate((pl.ds(128, 9 * 128), pl.ds(10 * 128, 7 * 128))):
        src = xin.at[1, :, lanes]
        far_halos.append(remote(src, xin.at[2 - far, :, lanes], halo_send.at[2 * i], halo_recv.at[2 * i], r.far))

    @pl.when(r.far_exists)
    def _():
        for cp in far_halos:
            cp.start()

    near_halo = remote(own_plane, xin.at[2 - near, :, body_lanes], halo_send.at[1], halo_recv.at[1], r.partner)
    near_halo.start()
    cot_copy = remote(cots.at[core], cots.at[core], cot_send, cot_recv, r.partner)
    cot_copy.start()

    lay_weights(wraw, wf, wb)
    for b in range(3):
        gs[b, 0:side, :] = jnp.zeros((side, 256), BF16)
        gs[b, side + cells : 2 * side + cells, :] = jnp.zeros((side, 256), BF16)
    lay_plane(xin, xk, 1)
    flip_plane(xk, xt, 1)
    near_halo.wait_recv()
    lay_plane(xin, xk, near)
    bias = bias_ref[...].reshape(1, 128)
    bias = jnp.concatenate([bias, bias], axis=1)
    for m in range(2):
        span = pl.ds(256 * m, 256)
        pre[span] = (
            bias
            + jnp.dot(xk[1, span], wf[1], preferred_element_type=F32)
            + jnp.dot(xk[near, span], wf[near], preferred_element_type=F32)
        )
    flip_plane(xk, xt, near)
    cot_copy.wait_recv()
    for half in range(2):
        for row in range(8):
            ctab[pl.ds(8 * half + row, 16, stride=16), :] = cots[half, row].astype(F32)

    pool_copies = []
    for m in range(4):
        if m % 2 == 0:
            pl.when(r.far_exists)(far_halos[m // 2].wait_recv)
            lay_plane(xin, xk, far, (m, m + 1))
            both = pl.ds(128 * m, 256)
            pre[both] = pre[both] + jnp.dot(xk[far, both], wf[far], preferred_element_type=F32)
        span = pl.ds(128 * m, 128)
        v = pre[span]
        s = 0.5 * jnp.tanh(0.5 * v) + 0.5
        z = v * s
        e = jnp.exp(z)
        act[span] = z
        pe[span] = e * (s * (1.0 + (v - z)))
        n = e * z
        sum_e[span] = e[:, :128] + e[:, 128:]
        sum_n[span] = n[:, :128] + n[:, 128:]
        half = pl.ds(64 * m, 64)
        even = pl.ds(128 * m, 64, stride=2)
        odd = pl.ds(128 * m + 1, 64, stride=2)
        sums[m, 0] = sum_e[even, :] + sum_e[odd, :]
        sums[m, 1] = sum_n[even, :] + sum_n[odd, :]
        cp = remote(sums.at[m], psums.at[m], pool_send.at[m], pool_recv.at[m], r.partner)
        cp.start()
        pool_copies.append(cp)
    flip_plane(xk, xt, far)
    row = lax.rem(lax.broadcasted_iota(jnp.int32, (128, 256), 0), side)
    bias_part = jnp.zeros((1, 256), F32)
    for m in range(4):
        pool_copies[m].wait_recv()
        den = sums[m, 0] + psums[m, 0]
        value = (sums[m, 1] + psums[m, 1]) / den
        half = pl.ds(64 * m, 64)
        pvt[half] = value
        cb = ctab[half] / den
        ca = cb * (1.0 - value)
        even = pl.ds(128 * m, 64, stride=2)
        odd = pl.ds(128 * m + 1, 64, stride=2)
        fa[even, :] = ca
        fa[odd, :] = ca
        fb[even, :] = cb
        fb[odd, :] = cb
        span = pl.ds(128 * m, 128)
        wide_a = jnp.concatenate([fa[span], fa[span]], axis=1)
        wide_b = jnp.concatenate([fb[span], fb[span]], axis=1)
        g = (pe[span] * (wide_a + wide_b * act[span])).astype(BF16)
        gs[1, side + 128 * m : side + 128 * m + 128, :] = g
        g = g.astype(F32)
        bias_part = bias_part + jnp.sum(g, axis=0, keepdims=True)
        after = jnp.where(row == side - 1, 0.0, pltpu.roll(g, 127, 0))
        before = jnp.where(row == 0, 0.0, pltpu.roll(g, 1, 0))
        gs[0, side + 128 * m : side + 128 * m + 128, :] = after.astype(BF16)
        gs[2, side + 128 * m : side + 128 * m + 128, :] = before.astype(BF16)

    half = pl.ds(pl.multiple_of(core * 32, 32), 32)
    far_half = pl.ds(pl.multiple_of(32 - core * 32, 32), 32)
    core_copies = []
    part[27] = jnp.zeros((64, 128), F32)
    part[27, 0:1, :] = bias_part[:, :128] + bias_part[:, 128:]
    rs_copies = []

    def pass_on(g):
        count = 3 if g < 8 else 4
        span = pl.ds(3 * g, count)
        core_copies[g].wait_recv()
        rows[span] = (part[span, half, :] + theirs[span].astype(F32)).astype(BF16)
        for piece in range(3 * g, 3 * g + count):
            who, slot = r.owner_of(piece)
            is_me = jnp.logical_and(r.owner, r.piece == piece)
            taps_of = rows.at[pl.ds(piece, 1)]
            cp = remote(taps_of, rs.at[slot], rs_send.at[piece], rs_recv, who)
            unless(is_me, cp.start, local(taps_of, rs.at[r.slot], rs_recv).start)
            rs_copies.append((is_me, cp))

    turned = xt[...].reshape(768, cells)
    for b in range(3):
        stack = jnp.dot(turned, gs[b, side : side + cells, :], preferred_element_type=F32)
        for a in range(3):
            g = b * 3 + a
            block = stack[256 * a : 256 * a + 256]
            part[3 * g] = block[192:256, :128] + block[0:64, 128:]
            part[3 * g + 1] = block[0:64, :128] + block[64:128, 128:]
            part[3 * g + 2] = block[64:128, :128] + block[128:192, 128:]
            span = pl.ds(3 * g, 3 if g < 8 else 4)
            mine[span] = part[span, far_half, :].astype(BF16)
            cp = remote(mine.at[span], theirs.at[span], core_send.at[g], core_recv.at[g], r.partner)
            cp.start()
            core_copies.append(cp)
        if b:
            for g in range(3 * b - 3, 3 * b):
                pass_on(g)
    for g in range(6, 9):
        pass_on(g)
    for m in range(4):
        at = 128 * m
        total = jnp.zeros((128, 384), F32)
        for b in range(3):
            wide = jnp.concatenate(
                [
                    gs[b, at : at + 128, 128:256],
                    gs[b, at + 32 : at + 160, :],
                    gs[b, at + 64 : at + 192, 0:128],
                ],
                axis=1,
            )
            total = total + lax.dot_general(
                wide, wb[b], (((1,), (1,)), ((), ())), preferred_element_type=F32
            )
        for a in range(3):
            bt[a, at : at + 128, :] = total[:, 128 * a : 128 * a + 128].astype(BF16)
    for row in range(8):
        pooled_out[row] = pvt[pl.ds(8 * core + row, 16, stride=16), :].astype(BF16)

    outs = [local(pooled_out, pooled_ref.at[0], out_sem.at[0])]
    outs[0].start()
    @pl.when(r.owner)
    def _():
        local(rs, rs, rs_recv).wait()
        total = rs[0].astype(F32)
        for i in range(1, 32):
            total = total + rs[i].astype(F32)
        ring_src[...] = total.astype(BF16)
        for i in range(7):
            cp = remote(ring_src, ring.at[r.ring_at], ring_send.at[i], ring_recv, r.ring_peer(i))
            cp.start()
        local(ring_src, ring.at[r.ring_at], ring_recv).start()

    bt_far = remote(bt.at[far], in_bt.at[far], bt_send.at[0], bt_recv.at[0], r.far)

    @pl.when(r.far_exists)
    def _():
        bt_far.start()

    bt_near = remote(bt.at[near], in_bt.at[near], bt_send.at[1], bt_recv.at[1], r.partner)
    bt_near.start()

    @pl.when(r.owner)
    def _():
        local(ring, ring, ring_recv).wait()
        total = ring[0].astype(F32)
        for i in range(1, 8):
            total = total + ring[i].astype(F32)
        final[...] = total.astype(BF16)
        place_of = gath.at[pl.ds(per_piece * r.piece, per_piece)]
        for i in range(31):
            cp = remote(final, place_of, ag_send.at[i], ag_recv.at[lax.div(r.piece, 7)], r.plane_peer(i))
            cp.start()
        local(final, place_of, ag_recv.at[lax.div(r.piece, 7)]).start()

    bt_near.wait()

    @pl.when(r.far_exists)
    def _():
        bt_far.wait()

    for q in range(pairs):
        span = pl.ds(side * q, side)
        summed = in_bt[0, span].astype(F32) + bt[1, span].astype(F32) + in_bt[2, span].astype(F32)
        input_grad_out[:, 128 * q : 128 * q + 128] = summed.astype(BF16)
    outs.append(local(input_grad_out, input_grad_ref.at[0, 0], out_sem.at[1]))
    outs[1].start()

    fw_copies = []
    for kind in range(4):
        span = gath.at[pl.ds(7 * kind, 7)]
        local(span, span, ag_recv.at[kind]).wait()
        cp = remote(span, sum_ref.at[core, pl.ds(7 * kind, 7)], fw_send.at[kind], fw_recv.at[kind], r.partner)
        cp.start()
        outs.append(local(span, sum_ref.at[core, pl.ds(7 * kind, 7)], out_sem.at[2 + kind]))
        outs[-1].start()
        fw_copies.append(cp)
    for kind in range(4):
        fw_copies[kind].wait()
    for cp in core_copies + pool_copies + [near_halo, cot_copy]:
        cp.wait_send()

    @pl.when(r.far_exists)
    def _():
        for cp in far_halos:
            cp.wait_send()

    for is_me, cp in rs_copies:
        unless(is_me, cp.wait_send)

    @pl.when(r.owner)
    def _():
        for i in range(7):
            local(ring_src, ring_src, ring_send.at[i]).wait()
        for i in range(31):
            local(final, final, ag_send.at[i]).wait()

    for cp in outs:
        cp.wait()


def hand_over(
    pooled, input_grad, total, pooled_ref, input_grad_ref, weight_ref, bias_ref, t, g, p, w, bias, get, put
):
    groups = (pl.ds(0, 9), pl.ds(9, 9), pl.ds(18, 10))
    reads = [local(total.at[:, span], t.at[:, span], get.at[i]) for i, span in enumerate(groups)]
    reads += [local(input_grad, g, get.at[3]), local(pooled, p, get.at[4])]
    for cp in reads:
        cp.start()
    writes = []
    for b in range(3):
        reads[b].wait()
        for a in range(3):
            first, at = 9 * b + 3 * a, 9 * a + 3 * b
            for h in range(2):
                w[at : at + 3, 32 * h : 32 * h + 32, :] = t[h, first : first + 3].astype(F32) * (1.0 / loss_scale)
            writes.append(local(w.at[pl.ds(at, 3)], weight_ref.at[pl.ds(at, 3)], put.at[3 * b + a]))
            writes[-1].start()
    bias[...] = t[0, taps, 0, :].astype(F32) * (1.0 / loss_scale)
    writes.append(local(bias, bias_ref, put.at[9]))
    writes[-1].start()
    reads[3].wait()
    writes.append(local(g, input_grad_ref, put.at[10]))
    writes[-1].start()
    reads[4].wait()
    writes.append(local(p, pooled_ref, put.at[11]))
    writes[-1].start()
    for cp in writes:
        cp.wait()


def block(volume, weight, conv_bias, cotangent):
    dma = pltpu.SemaphoreType.DMA
    vmem = pltpu.VMEM
    anywhere = pl.BlockSpec(memory_space=pltpu.HBM)
    shapes = (
        jax.ShapeDtypeStruct(cotangent.shape, BF16),
        jax.ShapeDtypeStruct(volume.shape, BF16),
        jax.ShapeDtypeStruct((taps, 64, 128), F32),
        jax.ShapeDtypeStruct(conv_bias.shape, F32),
    )
    sums = jax.ShapeDtypeStruct((2, blocks, 32, 128), BF16)
    results = pl.pallas_call(
        block_kernel,
        out_shape=shapes[:2] + (sums,),
        in_specs=[anywhere] * 4,
        out_specs=(anywhere,) * 3,
        scratch_shapes=[
            vmem((3, side, 2304), BF16),
            vmem((3, 3, 3, 64, 128), BF16),
            vmem((128,), F32),
            vmem((2, 8, 16, 128), BF16),
            vmem((3, 768, 256), BF16),
            vmem((3, 384, 512), BF16),
            vmem((3, cells, 768), BF16),
            vmem((3, 256, cells), BF16),
            vmem((cells, 256), F32),
            vmem((cells, 256), F32),
            vmem((cells, 256), F32),
            vmem((cells, 128), F32),
            vmem((cells, 128), F32),
            vmem((4, 2, 64, 128), F32),
            vmem((4, 2, 64, 128), F32),
            vmem((256, 128), F32),
            vmem((256, 128), F32),
            vmem((cells, 128), F32),
            vmem((cells, 128), F32),
            vmem((3, cells + 2 * side, 256), BF16),
            vmem((blocks, 64, 128), F32),
            vmem((3, cells, 128), BF16),
            vmem((3, cells, 128), BF16),
            vmem((blocks, 32, 128), BF16),
            vmem((blocks, 32, 128), BF16),
            vmem((blocks, 32, 128), BF16),
            vmem((32, per_piece, 32, 128), BF16),
            vmem((per_piece, 32, 128), BF16),
            vmem((8, per_piece, 32, 128), BF16),
            vmem((per_piece, 32, 128), BF16),
            vmem((blocks, 32, 128), BF16),
            vmem((8, 16, 128), BF16),
            vmem((side, 2048), BF16),
            dma((4,)), dma((3,)), dma((3,)), dma, dma, dma((4,)), dma((4,)), dma((2,)), dma((2,)),
            dma((9,)), dma((9,)), dma((pieces,)), dma, dma((8,)), dma, dma((32,)), dma((4,)), dma((4,)), dma((4,)), dma((6,)),
        ],
        compiler_params=pltpu.CompilerParams(
            collective_id=0, has_side_effects=True, vmem_limit_bytes=62 * 2**20
        ),
        name="conv_block",
    )(volume, weight, conv_bias, cotangent)
    pooled, input_grad, weight_grad, bias_grad = pl.pallas_call(
        hand_over,
        out_shape=shapes,
        in_specs=[anywhere] * 3,
        out_specs=(anywhere,) * 4,
        scratch_shapes=[vmem(v.shape, v.dtype) for v in (sums, shapes[1], shapes[0], shapes[2], shapes[3])]
        + [dma((5,)), dma((12,))],
        compiler_params=pltpu.CompilerParams(vmem_limit_bytes=62 * 2**20),
        name="hand_over",
    )(*results)
    return pooled, input_grad, weight_grad.reshape(weight.shape), bias_grad


def solution(mesh):
    placed = (P("sample", "space", None, None), P(), P(), P("sample", "space", None, None))
    return jax.shard_map(
        block,
        mesh=mesh,
        in_specs=placed,
        out_specs=(P("sample", "space", None, None), P("sample", "space", None, None), P(), P()),
        check_vma=False,
    )
```

```python
import jax
import jax.numpy as jnp
from jax import lax
from jax.experimental import pallas as pl
from jax.experimental.pallas import tpu as pltpu
from jax.sharding import PartitionSpec as P

MESH = pl.DeviceIdType.MESH
BF16 = jnp.bfloat16
F32 = jnp.float32
taps = 27
blocks = 28
per_piece = 1
pieces = blocks // per_piece
per_kind = pieces // 2
side = 32
pairs = 16
cells = 512
loss_scale = 256.0
spots = tuple((x, row) for row in (4, 3, 5, 2, 6, 1, 0) for x in (1, 0))


def place():
    space = lax.axis_index("space")
    sample = lax.axis_index("sample")
    core = lax.rem(space, 2)
    z_lo = lax.rem(lax.div(space, 2), 4)
    y = lax.div(space, 8)
    z = lax.div(sample, 4) * 4 + z_lo
    x = lax.rem(sample, 4)
    return x, y, z, core


def ident(x, y, z, core):
    return ((y * 4 + lax.rem(z, 4)) * 2 + core, lax.div(z, 4) * 4 + x)


class Reduce:
    def __init__(self):
        self.x, self.y, self.z, self.core = place()
        x, y, z = self.x, self.y, self.z
        self.kind_a = x < 2
        self.ring_at = jnp.where(self.kind_a, z, y)
        self.row_at = jnp.where(self.kind_a, y, z)
        self.kind = jnp.where(self.kind_a, 0, 1)
        side_x = jnp.where(self.kind_a, x, 3 - x)
        self.owner = False
        self.piece = 0
        for i, (sx, row) in enumerate(spots):
            here = jnp.logical_and(side_x == sx, self.row_at == row)
            self.owner = jnp.logical_or(self.owner, here)
            self.piece = self.piece + jnp.where(here, i, 0)
        self.piece = 2 * self.piece + self.kind
        self.slot = x * 8 + self.row_at
        self.partner = ident(x, y, z, 1 - self.core)
        plane = lax.axis_index("space")
        far_plane = plane + 2 * self.core - 1
        self.far_exists = jnp.logical_and(far_plane >= 0, far_plane < lax.axis_size("space"))
        self.far = (jnp.clip(far_plane, 0, lax.axis_size("space") - 1), lax.axis_index("sample"))
        self.near_tap = 2 - 2 * self.core
        self.far_tap = 2 * self.core

    def plane_peer(self, i):
        at = i + jnp.where(i >= self.row_at * 4 + self.x, 1, 0)
        row = lax.div(at, 4)
        y = jnp.where(self.kind_a, row, self.y)
        z = jnp.where(self.kind_a, self.z, row)
        return ident(lax.rem(at, 4), y, z, self.core)

    def ring_peer(self, i):
        at = i + jnp.where(i >= self.ring_at, 1, 0)
        y = jnp.where(self.kind_a, self.y, at)
        z = jnp.where(self.kind_a, at, self.z)
        return ident(self.x, y, z, self.core)

    def owner_of(self, piece):
        i, kind = divmod(piece, 2)
        x, row = spots[i]
        if kind == 0:
            return ident(x, row, self.z, self.core), self.x * 8 + self.y
        return ident(3 - x, self.y, row, self.core), self.x * 8 + self.z


def unless(me, action, otherwise=None):
    pl.when(jnp.logical_not(me))(action)
    if otherwise is not None:
        pl.when(me)(otherwise)


def signal(sem, who):
    pl.semaphore_signal(sem, inc=1, device_id=who, device_id_type=MESH)


def remote(src, dst, send, recv, who):
    return pltpu.make_async_remote_copy(
        src_ref=src, dst_ref=dst, send_sem=send, recv_sem=recv, device_id=who, device_id_type=MESH
    )


def local(src, dst, sem):
    return pltpu.make_async_copy(src, dst, sem)


def lay_weights(wraw, wf, wb):
    none = jnp.zeros((64, 128), BF16)
    for a in range(3):
        for b in range(3):
            t0, t1, t2 = (wraw[a, b, c] for c in range(3))
            for cell, column in enumerate(((t1, t2, none, t0), (t0, t1, t2, none))):
                for k, block in enumerate(column):
                    wf[a, 256 * b + 64 * k : 256 * b + 64 * k + 64, 128 * cell : 128 * cell + 128] = block
            for cell, row in enumerate(((t2, t1, t0, none), (none, t2, t1, t0))):
                at = (2 * a + cell) * 64
                for j, block in enumerate(row):
                    wb[b, at : at + 64, 128 * j : 128 * j + 128] = block


def lay_plane(xin, xk, p, chunks=range(4)):
    width = 512
    row = lax.broadcasted_iota(jnp.int32, (side, width), 0)
    low = lax.rem(lax.broadcasted_iota(jnp.int32, (side, width), 1), 128) < 64
    first, last = row == 0, row == side - 1
    for chunk in chunks:
        at = width * chunk
        left = xin[p, :, at : at + width].astype(F32)
        here = xin[p, :, at + 128 : at + 128 + width].astype(F32)
        right = xin[p, :, at + 256 : at + 256 + width].astype(F32)
        beside = jnp.where(low, right, left)
        for k, value in enumerate((here, beside)):
            up = jnp.where(first, 0.0, pltpu.roll(value, 1, 0))
            down = jnp.where(last, 0.0, pltpu.roll(value, side - 1, 0))
            for b, shifted in enumerate((up, value, down)):
                shifted = shifted.astype(BF16)
                for i in range(4):
                    q = 4 * chunk + i
                    lane = 256 * b + 128 * k
                    xk[p, side * q : side * q + side, lane : lane + 128] = shifted[:, 128 * i : 128 * i + 128]


def flip_plane(xk, xt, p):
    xt[p] = xk[p, :, 256:512].T


def block_kernel(
    volume_ref, weight_ref, bias_hbm, cot_ref,
    pooled_ref, input_grad_ref, sum_ref,
    xin, wraw, bias_ref, cots, wf, wb, xk, xt, pre, act, pe, sum_e, sum_n, sums, psums, ctab, pvt, fa, fb, gs, part, bt, in_bt,
    mine, theirs, rows, rs, ring_src, ring, final,
    gath, pooled_out, input_grad_out,
    load_sem, halo_send, halo_recv, cot_send, cot_recv, pool_send, pool_recv, bt_send, bt_recv,
    core_send, core_recv, rs_send, rs_recv, ring_send, ring_recv, ag_send, ag_recv, fw_send, fw_recv, out_sem,
):
    r = Reduce()
    core = r.core
    near, far = r.near_tap, r.far_tap
    body_lanes = pl.ds(128, 2048)
    bar = pltpu.get_barrier_semaphore()

    @pl.when(r.far_exists)
    def _():
        signal(bar, r.far)

    signal(bar, r.partner)
    loads = [
        local(volume_ref.at[0, 0], xin.at[1, :, body_lanes], load_sem.at[0]),
        local(cot_ref.at[0], cots.at[core], load_sem.at[1]),
        local(weight_ref, wraw, load_sem.at[2]),
        local(bias_hbm, bias_ref, load_sem.at[3]),
    ]
    for cp in loads:
        cp.start()

    @pl.when(r.owner)
    def _():
        for i in reversed(range(31)):
            signal(bar, r.plane_peer(i))
        for i in range(7):
            signal(bar, r.ring_peer(i))

    for p in range(3):
        xin[p, :, 0:128] = jnp.zeros((side, 128), BF16)
        xin[p, :, 2176:2304] = jnp.zeros((side, 128), BF16)

    @pl.when(jnp.logical_not(r.far_exists))
    def _():
        xin[far] = jnp.zeros((side, 2304), BF16)
        in_bt[2 - far] = jnp.zeros((cells, 128), BF16)

    for cp in loads:
        cp.wait()
    own = jnp.where(r.owner, 1, 0)
    pl.semaphore_wait(bar, pieces + 1 + 6 * own + jnp.where(r.far_exists, 1, 0))

    own_plane = xin.at[1, :, body_lanes]
    far_halos = []
    for i, lanes in enumerate((pl.ds(128, 9 * 128), pl.ds(10 * 128, 7 * 128))):
        src = xin.at[1, :, lanes]
        far_halos.append(remote(src, xin.at[2 - far, :, lanes], halo_send.at[2 * i], halo_recv.at[2 * i], r.far))

    @pl.when(r.far_exists)
    def _():
        for cp in far_halos:
            cp.start()

    near_halo = remote(own_plane, xin.at[2 - near, :, body_lanes], halo_send.at[1], halo_recv.at[1], r.partner)
    near_halo.start()
    cot_copy = remote(cots.at[core], cots.at[core], cot_send, cot_recv, r.partner)
    cot_copy.start()

    lay_weights(wraw, wf, wb)
    for b in range(3):
        gs[b, 0:side, :] = jnp.zeros((side, 256), BF16)
        gs[b, side + cells : 2 * side + cells, :] = jnp.zeros((side, 256), BF16)
    lay_plane(xin, xk, 1)
    flip_plane(xk, xt, 1)
    near_halo.wait_recv()
    lay_plane(xin, xk, near)
    bias = bias_ref[...].reshape(1, 128)
    bias = jnp.concatenate([bias, bias], axis=1)
    for m in range(2):
        span = pl.ds(256 * m, 256)
        pre[span] = (
            bias
            + jnp.dot(xk[1, span], wf[1], preferred_element_type=F32)
            + jnp.dot(xk[near, span], wf[near], preferred_element_type=F32)
        )
    flip_plane(xk, xt, near)
    cot_copy.wait_recv()
    for half in range(2):
        for row in range(8):
            ctab[pl.ds(8 * half + row, 16, stride=16), :] = cots[half, row].astype(F32)

    pool_copies = []
    for m in range(4):
        if m % 2 == 0:
            pl.when(r.far_exists)(far_halos[m // 2].wait_recv)
            lay_plane(xin, xk, far, (m, m + 1))
            both = pl.ds(128 * m, 256)
            pre[both] = pre[both] + jnp.dot(xk[far, both], wf[far], preferred_element_type=F32)
        span = pl.ds(128 * m, 128)
        v = pre[span]
        s = 0.5 * jnp.tanh(0.5 * v) + 0.5
        z = v * s
        e = jnp.exp(z)
        act[span] = z
        pe[span] = e * (s * (1.0 + (v - z)))
        n = e * z
        sum_e[span] = e[:, :128] + e[:, 128:]
        sum_n[span] = n[:, :128] + n[:, 128:]
        half = pl.ds(64 * m, 64)
        even = pl.ds(128 * m, 64, stride=2)
        odd = pl.ds(128 * m + 1, 64, stride=2)
        sums[m, 0] = sum_e[even, :] + sum_e[odd, :]
        sums[m, 1] = sum_n[even, :] + sum_n[odd, :]
        cp = remote(sums.at[m], psums.at[m], pool_send.at[m], pool_recv.at[m], r.partner)
        cp.start()
        pool_copies.append(cp)
    flip_plane(xk, xt, far)
    row = lax.rem(lax.broadcasted_iota(jnp.int32, (128, 256), 0), side)
    bias_part = jnp.zeros((1, 256), F32)
    for m in range(4):
        pool_copies[m].wait_recv()
        den = sums[m, 0] + psums[m, 0]
        value = (sums[m, 1] + psums[m, 1]) / den
        half = pl.ds(64 * m, 64)
        pvt[half] = value
        cb = ctab[half] / den
        ca = cb * (1.0 - value)
        even = pl.ds(128 * m, 64, stride=2)
        odd = pl.ds(128 * m + 1, 64, stride=2)
        fa[even, :] = ca
        fa[odd, :] = ca
        fb[even, :] = cb
        fb[odd, :] = cb
        span = pl.ds(128 * m, 128)
        wide_a = jnp.concatenate([fa[span], fa[span]], axis=1)
        wide_b = jnp.concatenate([fb[span], fb[span]], axis=1)
        g = (pe[span] * (wide_a + wide_b * act[span])).astype(BF16)
        gs[1, side + 128 * m : side + 128 * m + 128, :] = g
        g = g.astype(F32)
        bias_part = bias_part + jnp.sum(g, axis=0, keepdims=True)
        after = jnp.where(row == side - 1, 0.0, pltpu.roll(g, 127, 0))
        before = jnp.where(row == 0, 0.0, pltpu.roll(g, 1, 0))
        gs[0, side + 128 * m : side + 128 * m + 128, :] = after.astype(BF16)
        gs[2, side + 128 * m : side + 128 * m + 128, :] = before.astype(BF16)

    half = pl.ds(pl.multiple_of(core * 32, 32), 32)
    far_half = pl.ds(pl.multiple_of(32 - core * 32, 32), 32)
    core_copies = []
    part[27] = jnp.zeros((64, 128), F32)
    part[27, 0:1, :] = bias_part[:, :128] + bias_part[:, 128:]
    rs_copies = []

    def pass_on(g):
        count = 3 if g < 8 else 4
        span = pl.ds(3 * g, count)
        core_copies[g].wait_recv()
        rows[span] = (part[span, half, :] + theirs[span].astype(F32)).astype(BF16)
        for piece in range(3 * g, 3 * g + count):
            who, slot = r.owner_of(piece)
            is_me = jnp.logical_and(r.owner, r.piece == piece)
            taps_of = rows.at[pl.ds(piece, 1)]
            cp = remote(taps_of, rs.at[slot], rs_send.at[piece], rs_recv, who)
            unless(is_me, cp.start, local(taps_of, rs.at[r.slot], rs_recv).start)
            rs_copies.append((is_me, cp))

    turned = xt[...].reshape(768, cells)
    for b in range(3):
        stack = jnp.dot(turned, gs[b, side : side + cells, :], preferred_element_type=F32)
        for a in range(3):
            g = b * 3 + a
            block = stack[256 * a : 256 * a + 256]
            part[3 * g] = block[192:256, :128] + block[0:64, 128:]
            part[3 * g + 1] = block[0:64, :128] + block[64:128, 128:]
            part[3 * g + 2] = block[64:128, :128] + block[128:192, 128:]
            span = pl.ds(3 * g, 3 if g < 8 else 4)
            mine[span] = part[span, far_half, :].astype(BF16)
            cp = remote(mine.at[span], theirs.at[span], core_send.at[g], core_recv.at[g], r.partner)
            cp.start()
            core_copies.append(cp)
        if b:
            for g in range(3 * b - 3, 3 * b):
                pass_on(g)
    for g in range(6, 9):
        pass_on(g)
    for m in range(4):
        at = 128 * m
        total = jnp.zeros((128, 384), F32)
        for b in range(3):
            wide = jnp.concatenate(
                [
                    gs[b, at : at + 128, 128:256],
                    gs[b, at + 32 : at + 160, :],
                    gs[b, at + 64 : at + 192, 0:128],
                ],
                axis=1,
            )
            total = total + lax.dot_general(
                wide, wb[b], (((1,), (1,)), ((), ())), preferred_element_type=F32
            )
        for a in range(3):
            bt[a, at : at + 128, :] = total[:, 128 * a : 128 * a + 128].astype(BF16)
    for row in range(8):
        pooled_out[row] = pvt[pl.ds(8 * core + row, 16, stride=16), :].astype(BF16)

    outs = [local(pooled_out, pooled_ref.at[0], out_sem.at[0])]
    outs[0].start()
    @pl.when(r.owner)
    def _():
        local(rs, rs, rs_recv).wait()
        total = rs[0].astype(F32)
        for i in range(1, 32):
            total = total + rs[i].astype(F32)
        ring_src[...] = total.astype(BF16)
        for i in range(7):
            cp = remote(ring_src, ring.at[r.ring_at], ring_send.at[i], ring_recv, r.ring_peer(i))
            cp.start()
        local(ring_src, ring.at[r.ring_at], ring_recv).start()

    bt_far = remote(bt.at[far], in_bt.at[far], bt_send.at[0], bt_recv.at[0], r.far)

    @pl.when(r.far_exists)
    def _():
        bt_far.start()

    bt_near = remote(bt.at[near], in_bt.at[near], bt_send.at[1], bt_recv.at[1], r.partner)
    bt_near.start()

    @pl.when(r.owner)
    def _():
        local(ring, ring, ring_recv).wait()
        total = ring[0].astype(F32)
        for i in range(1, 8):
            total = total + ring[i].astype(F32)
        final[...] = total.astype(BF16)
        place_of = gath.at[pl.ds(per_piece * r.piece, per_piece)]
        for i in range(31):
            cp = remote(final, place_of, ag_send.at[i], ag_recv.at[lax.div(r.piece, 7)], r.plane_peer(i))
            cp.start()
        local(final, place_of, ag_recv.at[lax.div(r.piece, 7)]).start()

    bt_near.wait()

    @pl.when(r.far_exists)
    def _():
        bt_far.wait()

    for q in range(pairs):
        span = pl.ds(side * q, side)
        summed = in_bt[0, span].astype(F32) + bt[1, span].astype(F32) + in_bt[2, span].astype(F32)
        input_grad_out[:, 128 * q : 128 * q + 128] = summed.astype(BF16)
    outs.append(local(input_grad_out, input_grad_ref.at[0, 0], out_sem.at[1]))
    outs[1].start()

    fw_copies = []
    for kind in range(4):
        span = gath.at[pl.ds(7 * kind, 7)]
        local(span, span, ag_recv.at[kind]).wait()
        cp = remote(span, sum_ref.at[core, pl.ds(7 * kind, 7)], fw_send.at[kind], fw_recv.at[kind], r.partner)
        cp.start()
        outs.append(local(span, sum_ref.at[core, pl.ds(7 * kind, 7)], out_sem.at[2 + kind]))
        outs[-1].start()
        fw_copies.append(cp)
    for kind in range(4):
        fw_copies[kind].wait()
    for cp in core_copies + pool_copies + [near_halo, cot_copy]:
        cp.wait_send()

    @pl.when(r.far_exists)
    def _():
        for cp in far_halos:
            cp.wait_send()

    for is_me, cp in rs_copies:
        unless(is_me, cp.wait_send)

    @pl.when(r.owner)
    def _():
        for i in range(7):
            local(ring_src, ring_src, ring_send.at[i]).wait()
        for i in range(31):
            local(final, final, ag_send.at[i]).wait()

    for cp in outs:
        cp.wait()


def hand_over(
    pooled, input_grad, total, pooled_ref, input_grad_ref, weight_ref, bias_ref, t, g, p, w, bias, get, put
):
    groups = (pl.ds(0, 9), pl.ds(9, 9), pl.ds(18, 10))
    reads = [local(total.at[:, span], t.at[:, span], get.at[i]) for i, span in enumerate(groups)]
    reads += [local(input_grad, g, get.at[3]), local(pooled, p, get.at[4])]
    for cp in reads:
        cp.start()
    writes = []
    for b in range(3):
        reads[b].wait()
        for a in range(3):
            first, at = 9 * b + 3 * a, 9 * a + 3 * b
            for h in range(2):
                w[at : at + 3, 32 * h : 32 * h + 32, :] = t[h, first : first + 3].astype(F32) * (1.0 / loss_scale)
            writes.append(local(w.at[pl.ds(at, 3)], weight_ref.at[pl.ds(at, 3)], put.at[3 * b + a]))
            writes[-1].start()
    bias[...] = t[0, taps, 0, :].astype(F32) * (1.0 / loss_scale)
    writes.append(local(bias, bias_ref, put.at[9]))
    writes[-1].start()
    reads[3].wait()
    writes.append(local(g, input_grad_ref, put.at[10]))
    writes[-1].start()
    reads[4].wait()
    writes.append(local(p, pooled_ref, put.at[11]))
    writes[-1].start()
    for cp in writes:
        cp.wait()


def block(volume, weight, conv_bias, cotangent):
    dma = pltpu.SemaphoreType.DMA
    vmem = pltpu.VMEM
    anywhere = pl.BlockSpec(memory_space=pltpu.HBM)
    shapes = (
        jax.ShapeDtypeStruct(cotangent.shape, BF16),
        jax.ShapeDtypeStruct(volume.shape, BF16),
        jax.ShapeDtypeStruct((taps, 64, 128), F32),
        jax.ShapeDtypeStruct(conv_bias.shape, F32),
    )
    sums = jax.ShapeDtypeStruct((2, blocks, 32, 128), BF16)
    results = pl.pallas_call(
        block_kernel,
        out_shape=shapes[:2] + (sums,),
        in_specs=[anywhere] * 4,
        out_specs=(anywhere,) * 3,
        scratch_shapes=[
            vmem((3, side, 2304), BF16),
            vmem((3, 3, 3, 64, 128), BF16),
            vmem((128,), F32),
            vmem((2, 8, 16, 128), BF16),
            vmem((3, 768, 256), BF16),
            vmem((3, 384, 512), BF16),
            vmem((3, cells, 768), BF16),
            vmem((3, 256, cells), BF16),
            vmem((cells, 256), F32),
            vmem((cells, 256), F32),
            vmem((cells, 256), F32),
            vmem((cells + 8, 128), F32),
            vmem((cells + 8, 128), F32),
            vmem((4, 2, 64, 128), F32),
            vmem((4, 2, 64, 128), F32),
            vmem((272, 128), F32),
            vmem((272, 128), F32),
            vmem((cells + 8, 128), F32),
            vmem((cells + 8, 128), F32),
            vmem((3, cells + 2 * side, 256), BF16),
            vmem((blocks, 64, 128), F32),
            vmem((3, cells, 128), BF16),
            vmem((3, cells, 128), BF16),
            vmem((blocks, 32, 128), BF16),
            vmem((blocks, 32, 128), BF16),
            vmem((blocks, 32, 128), BF16),
            vmem((32, per_piece, 32, 128), BF16),
            vmem((per_piece, 32, 128), BF16),
            vmem((8, per_piece, 32, 128), BF16),
            vmem((per_piece, 32, 128), BF16),
            vmem((blocks, 32, 128), BF16),
            vmem((8, 16, 128), BF16),
            vmem((side, 2048), BF16),
            dma((4,)), dma((3,)), dma((3,)), dma, dma, dma((4,)), dma((4,)), dma((2,)), dma((2,)),
            dma((9,)), dma((9,)), dma((pieces,)), dma, dma((8,)), dma, dma((32,)), dma((4,)), dma((4,)), dma((4,)), dma((6,)),
        ],
        compiler_params=pltpu.CompilerParams(
            collective_id=0, has_side_effects=True, vmem_limit_bytes=62 * 2**20
        ),
        name="conv_block",
    )(volume, weight, conv_bias, cotangent)
    pooled, input_grad, weight_grad, bias_grad = pl.pallas_call(
        hand_over,
        out_shape=shapes,
        in_specs=[anywhere] * 3,
        out_specs=(anywhere,) * 4,
        scratch_shapes=[vmem(v.shape, v.dtype) for v in (sums, shapes[1], shapes[0], shapes[2], shapes[3])]
        + [dma((5,)), dma((12,))],
        compiler_params=pltpu.CompilerParams(vmem_limit_bytes=62 * 2**20),
        name="hand_over",
    )(*results)
    return pooled, input_grad, weight_grad.reshape(weight.shape), bias_grad


def solution(mesh):
    placed = (P("sample", "space", None, None), P(), P(), P("sample", "space", None, None))
    return jax.shard_map(
        block,
        mesh=mesh,
        in_specs=placed,
        out_specs=(P("sample", "space", None, None), P("sample", "space", None, None), P(), P()),
        check_vma=False,
    )
```

```python
import jax
import jax.numpy as jnp
from jax import lax
from jax.experimental import pallas as pl
from jax.experimental.pallas import tpu as pltpu
from jax.sharding import PartitionSpec as P

MESH = pl.DeviceIdType.MESH
BF16 = jnp.bfloat16
F32 = jnp.float32
taps = 27
blocks = 28
per_piece = 1
pieces = blocks // per_piece
per_kind = pieces // 2
side = 32
pairs = 16
cells = 512
loss_scale = 256.0
spots = tuple((x, row) for row in (4, 3, 5, 2, 6, 1, 0) for x in (1, 0))


def place():
    space = lax.axis_index("space")
    sample = lax.axis_index("sample")
    core = lax.rem(space, 2)
    z_lo = lax.rem(lax.div(space, 2), 4)
    y = lax.div(space, 8)
    z = lax.div(sample, 4) * 4 + z_lo
    x = lax.rem(sample, 4)
    return x, y, z, core


def ident(x, y, z, core):
    return ((y * 4 + lax.rem(z, 4)) * 2 + core, lax.div(z, 4) * 4 + x)


class Reduce:
    def __init__(self):
        self.x, self.y, self.z, self.core = place()
        x, y, z = self.x, self.y, self.z
        self.kind_a = x < 2
        self.ring_at = jnp.where(self.kind_a, z, y)
        self.row_at = jnp.where(self.kind_a, y, z)
        self.kind = jnp.where(self.kind_a, 0, 1)
        side_x = jnp.where(self.kind_a, x, 3 - x)
        self.owner = False
        self.piece = 0
        for i, (sx, row) in enumerate(spots):
            here = jnp.logical_and(side_x == sx, self.row_at == row)
            self.owner = jnp.logical_or(self.owner, here)
            self.piece = self.piece + jnp.where(here, i, 0)
        self.piece = 2 * self.piece + self.kind
        self.slot = x * 8 + self.row_at
        self.partner = ident(x, y, z, 1 - self.core)
        plane = lax.axis_index("space")
        far_plane = plane + 2 * self.core - 1
        self.far_exists = jnp.logical_and(far_plane >= 0, far_plane < lax.axis_size("space"))
        self.far = (jnp.clip(far_plane, 0, lax.axis_size("space") - 1), lax.axis_index("sample"))
        self.near_tap = 2 - 2 * self.core
        self.far_tap = 2 * self.core

    def plane_peer(self, i):
        at = i + jnp.where(i >= self.row_at * 4 + self.x, 1, 0)
        row = lax.div(at, 4)
        y = jnp.where(self.kind_a, row, self.y)
        z = jnp.where(self.kind_a, self.z, row)
        return ident(lax.rem(at, 4), y, z, self.core)

    def ring_peer(self, i):
        at = i + jnp.where(i >= self.ring_at, 1, 0)
        y = jnp.where(self.kind_a, self.y, at)
        z = jnp.where(self.kind_a, at, self.z)
        return ident(self.x, y, z, self.core)

    def owner_of(self, piece):
        i, kind = divmod(piece, 2)
        x, row = spots[i]
        if kind == 0:
            return ident(x, row, self.z, self.core), self.x * 8 + self.y
        return ident(3 - x, self.y, row, self.core), self.x * 8 + self.z


def unless(me, action, otherwise=None):
    pl.when(jnp.logical_not(me))(action)
    if otherwise is not None:
        pl.when(me)(otherwise)


def signal(sem, who):
    pl.semaphore_signal(sem, inc=1, device_id=who, device_id_type=MESH)


def remote(src, dst, send, recv, who):
    return pltpu.make_async_remote_copy(
        src_ref=src, dst_ref=dst, send_sem=send, recv_sem=recv, device_id=who, device_id_type=MESH
    )


def local(src, dst, sem):
    return pltpu.make_async_copy(src, dst, sem)


def lay_weights(wraw, wf, wb):
    none = jnp.zeros((64, 128), BF16)
    for a in range(3):
        for b in range(3):
            t0, t1, t2 = (wraw[a, b, c] for c in range(3))
            for cell, column in enumerate(((t1, t2, none, t0), (t0, t1, t2, none))):
                for k, block in enumerate(column):
                    wf[a, 256 * b + 64 * k : 256 * b + 64 * k + 64, 128 * cell : 128 * cell + 128] = block
            for cell, row in enumerate(((t2, t1, t0, none), (none, t2, t1, t0))):
                at = (2 * a + cell) * 64
                for j, block in enumerate(row):
                    wb[b, at : at + 64, 128 * j : 128 * j + 128] = block


def lay_plane(xin, xk, p, chunks=range(4)):
    width = 512
    row = lax.broadcasted_iota(jnp.int32, (side, width), 0)
    low = lax.rem(lax.broadcasted_iota(jnp.int32, (side, width), 1), 128) < 64
    first, last = row == 0, row == side - 1
    for chunk in chunks:
        at = width * chunk
        left = xin[p, :, at : at + width].astype(F32)
        here = xin[p, :, at + 128 : at + 128 + width].astype(F32)
        right = xin[p, :, at + 256 : at + 256 + width].astype(F32)
        beside = jnp.where(low, right, left)
        for k, value in enumerate((here, beside)):
            up = jnp.where(first, 0.0, pltpu.roll(value, 1, 0))
            down = jnp.where(last, 0.0, pltpu.roll(value, side - 1, 0))
            for b, shifted in enumerate((up, value, down)):
                shifted = shifted.astype(BF16)
                for i in range(4):
                    q = 4 * chunk + i
                    lane = 256 * b + 128 * k
                    xk[p, side * q : side * q + side, lane : lane + 128] = shifted[:, 128 * i : 128 * i + 128]


def flip_plane(xk, xt, p):
    xt[p] = xk[p, :, 256:512].T


def block_kernel(
    volume_ref, weight_ref, bias_hbm, cot_ref,
    pooled_ref, input_grad_ref, sum_ref,
    xin, wraw, bias_ref, cots, wf, wb, xk, xt, pre, act, pe, sum_e, sum_n, sums, psums, ctab, pvt, fa, fb, gs, part, bt, in_bt,
    mine, theirs, rows, rs, ring_src, ring, final,
    gath, pooled_out, input_grad_out,
    load_sem, halo_send, halo_recv, cot_send, cot_recv, pool_send, pool_recv, bt_send, bt_recv,
    core_send, core_recv, rs_send, rs_recv, ring_send, ring_recv, ag_send, ag_recv, fw_send, fw_recv, out_sem,
):
    r = Reduce()
    core = r.core
    near, far = r.near_tap, r.far_tap
    body_lanes = pl.ds(128, 2048)
    bar = pltpu.get_barrier_semaphore()

    @pl.when(r.far_exists)
    def _():
        signal(bar, r.far)

    signal(bar, r.partner)
    loads = [
        local(volume_ref.at[0, 0], xin.at[1, :, body_lanes], load_sem.at[0]),
        local(cot_ref.at[0], cots.at[core], load_sem.at[1]),
        local(weight_ref, wraw, load_sem.at[2]),
        local(bias_hbm, bias_ref, load_sem.at[3]),
    ]
    for cp in loads:
        cp.start()

    @pl.when(r.owner)
    def _():
        for i in reversed(range(31)):
            signal(bar, r.plane_peer(i))
        for i in range(7):
            signal(bar, r.ring_peer(i))

    for p in range(3):
        xin[p, :, 0:128] = jnp.zeros((side, 128), BF16)
        xin[p, :, 2176:2304] = jnp.zeros((side, 128), BF16)

    @pl.when(jnp.logical_not(r.far_exists))
    def _():
        xin[far] = jnp.zeros((side, 2304), BF16)
        in_bt[2 - far] = jnp.zeros((cells, 128), BF16)

    for cp in loads:
        cp.wait()
    own = jnp.where(r.owner, 1, 0)
    pl.semaphore_wait(bar, pieces + 1 + 6 * own + jnp.where(r.far_exists, 1, 0))

    own_plane = xin.at[1, :, body_lanes]
    far_halos = []
    for i, lanes in enumerate((pl.ds(128, 9 * 128), pl.ds(10 * 128, 7 * 128))):
        src = xin.at[1, :, lanes]
        far_halos.append(remote(src, xin.at[2 - far, :, lanes], halo_send.at[2 * i], halo_recv.at[2 * i], r.far))

    @pl.when(r.far_exists)
    def _():
        for cp in far_halos:
            cp.start()

    near_halo = remote(own_plane, xin.at[2 - near, :, body_lanes], halo_send.at[1], halo_recv.at[1], r.partner)
    near_halo.start()
    cot_copy = remote(cots.at[core], cots.at[core], cot_send, cot_recv, r.partner)
    cot_copy.start()

    lay_weights(wraw, wf, wb)
    for b in range(3):
        gs[b, 0:side, :] = jnp.zeros((side, 256), BF16)
        gs[b, side + cells : 2 * side + cells, :] = jnp.zeros((side, 256), BF16)
    lay_plane(xin, xk, 1)
    flip_plane(xk, xt, 1)
    near_halo.wait_recv()
    lay_plane(xin, xk, near)
    bias = bias_ref[...].reshape(1, 128)
    bias = jnp.concatenate([bias, bias], axis=1)
    for m in range(2):
        span = pl.ds(256 * m, 256)
        pre[span] = (
            bias
            + jnp.dot(xk[1, span], wf[1], preferred_element_type=F32)
            + jnp.dot(xk[near, span], wf[near], preferred_element_type=F32)
        )
    flip_plane(xk, xt, near)
    cot_copy.wait_recv()
    for half in range(2):
        for row in range(8):
            ctab[pl.ds(8 * half + row, 16, stride=16), :] = cots[half, row].astype(F32)

    pool_copies = []
    for m in range(4):
        if m % 2 == 0:
            pl.when(r.far_exists)(far_halos[m // 2].wait_recv)
            lay_plane(xin, xk, far, (m, m + 1))
            both = pl.ds(128 * m, 256)
            pre[both] = pre[both] + jnp.dot(xk[far, both], wf[far], preferred_element_type=F32)
        span = pl.ds(128 * m, 128)
        v = pre[span]
        s = 0.5 * jnp.tanh(0.5 * v) + 0.5
        z = v * s
        e = jnp.exp(z)
        act[span] = z
        pe[span] = e * (s * (1.0 + (v - z)))
        n = e * z
        sum_e[span] = e[:, :128] + e[:, 128:]
        sum_n[span] = n[:, :128] + n[:, 128:]
        half = pl.ds(64 * m, 64)
        even = pl.ds(128 * m, 64, stride=2)
        odd = pl.ds(128 * m + 1, 64, stride=2)
        sums[m, 0] = sum_e[even, :] + sum_e[odd, :]
        sums[m, 1] = sum_n[even, :] + sum_n[odd, :]
        cp = remote(sums.at[m], psums.at[m], pool_send.at[m], pool_recv.at[m], r.partner)
        cp.start()
        pool_copies.append(cp)
    flip_plane(xk, xt, far)
    row = lax.rem(lax.broadcasted_iota(jnp.int32, (128, 256), 0), side)
    bias_part = jnp.zeros((1, 256), F32)
    for m in range(4):
        pool_copies[m].wait_recv()
        den = sums[m, 0] + psums[m, 0]
        value = (sums[m, 1] + psums[m, 1]) / den
        half = pl.ds(64 * m, 64)
        pvt[half] = value
        cb = ctab[half] / den
        ca = cb * (1.0 - value)
        even = pl.ds(128 * m, 64, stride=2)
        odd = pl.ds(128 * m + 1, 64, stride=2)
        fa[even, :] = ca
        fa[odd, :] = ca
        fb[even, :] = cb
        fb[odd, :] = cb
        span = pl.ds(128 * m, 128)
        wide_a = jnp.concatenate([fa[span], fa[span]], axis=1)
        wide_b = jnp.concatenate([fb[span], fb[span]], axis=1)
        g = (pe[span] * (wide_a + wide_b * act[span])).astype(BF16)
        gs[1, side + 128 * m : side + 128 * m + 128, :] = g
        g = g.astype(F32)
        bias_part = bias_part + jnp.sum(g, axis=0, keepdims=True)
        after = jnp.where(row == side - 1, 0.0, pltpu.roll(g, 127, 0))
        before = jnp.where(row == 0, 0.0, pltpu.roll(g, 1, 0))
        gs[0, side + 128 * m : side + 128 * m + 128, :] = after.astype(BF16)
        gs[2, side + 128 * m : side + 128 * m + 128, :] = before.astype(BF16)

    half = pl.ds(pl.multiple_of(core * 32, 32), 32)
    far_half = pl.ds(pl.multiple_of(32 - core * 32, 32), 32)
    core_copies = []
    part[27] = jnp.zeros((64, 128), F32)
    part[27, 0:1, :] = bias_part[:, :128] + bias_part[:, 128:]
    rs_copies = []

    def pass_on(g):
        count = 3 if g < 8 else 4
        span = pl.ds(3 * g, count)
        core_copies[g].wait_recv()
        rows[span] = (part[span, half, :] + theirs[span].astype(F32)).astype(BF16)
        for piece in range(3 * g, 3 * g + count):
            who, slot = r.owner_of(piece)
            is_me = jnp.logical_and(r.owner, r.piece == piece)
            taps_of = rows.at[pl.ds(piece, 1)]
            cp = remote(taps_of, rs.at[slot], rs_send.at[piece], rs_recv, who)
            unless(is_me, cp.start, local(taps_of, rs.at[r.slot], rs_recv).start)
            rs_copies.append((is_me, cp))

    turned = xt[...].reshape(768, cells)
    for b in range(3):
        stack = jnp.dot(turned, gs[b, side : side + cells, :], preferred_element_type=F32)
        for a in range(3):
            g = b * 3 + a
            block = stack[256 * a : 256 * a + 256]
            part[3 * g] = block[192:256, :128] + block[0:64, 128:]
            part[3 * g + 1] = block[0:64, :128] + block[64:128, 128:]
            part[3 * g + 2] = block[64:128, :128] + block[128:192, 128:]
            span = pl.ds(3 * g, 3 if g < 8 else 4)
            mine[span] = part[span, far_half, :].astype(BF16)
            cp = remote(mine.at[span], theirs.at[span], core_send.at[g], core_recv.at[g], r.partner)
            cp.start()
            core_copies.append(cp)
        if b:
            for g in range(3 * b - 3, 3 * b):
                pass_on(g)
    for g in range(6, 9):
        pass_on(g)
    for m in range(4):
        at = 128 * m
        total = jnp.zeros((128, 384), F32)
        for b in range(3):
            wide = jnp.concatenate(
                [
                    gs[b, at : at + 128, 128:256],
                    gs[b, at + 32 : at + 160, :],
                    gs[b, at + 64 : at + 192, 0:128],
                ],
                axis=1,
            )
            total = total + lax.dot_general(
                wide, wb[b], (((1,), (1,)), ((), ())), preferred_element_type=F32
            )
        for a in range(3):
            bt[a, at : at + 128, :] = total[:, 128 * a : 128 * a + 128].astype(BF16)
    for row in range(8):
        pooled_out[row] = pvt[pl.ds(8 * core + row, 16, stride=16), :].astype(BF16)

    outs = [local(pooled_out, pooled_ref.at[0], out_sem.at[0])]
    outs[0].start()
    @pl.when(r.owner)
    def _():
        local(rs, rs, rs_recv).wait()
        total = rs[0].astype(F32)
        for i in range(1, 32):
            total = total + rs[i].astype(F32)
        ring_src[...] = total.astype(BF16)
        for i in range(7):
            cp = remote(ring_src, ring.at[r.ring_at], ring_send.at[i], ring_recv, r.ring_peer(i))
            cp.start()
        local(ring_src, ring.at[r.ring_at], ring_recv).start()

    bt_far = remote(bt.at[far], in_bt.at[far], bt_send.at[0], bt_recv.at[0], r.far)

    @pl.when(r.far_exists)
    def _():
        bt_far.start()

    bt_near = remote(bt.at[near], in_bt.at[near], bt_send.at[1], bt_recv.at[1], r.partner)
    bt_near.start()

    @pl.when(r.owner)
    def _():
        plane_peers = [r.plane_peer(i) for i in range(31)]
        local(ring, ring, ring_recv).wait()
        total = ring[0].astype(F32)
        for i in range(1, 8):
            total = total + ring[i].astype(F32)
        final[...] = total.astype(BF16)
        place_of = gath.at[pl.ds(per_piece * r.piece, per_piece)]
        for i in range(31):
            cp = remote(final, place_of, ag_send.at[i], ag_recv.at[lax.div(r.piece, 7)], plane_peers[i])
            cp.start()
        local(final, place_of, ag_recv.at[lax.div(r.piece, 7)]).start()

    bt_near.wait()

    @pl.when(r.far_exists)
    def _():
        bt_far.wait()

    for q in range(pairs):
        span = pl.ds(side * q, side)
        summed = in_bt[0, span].astype(F32) + bt[1, span].astype(F32) + in_bt[2, span].astype(F32)
        input_grad_out[:, 128 * q : 128 * q + 128] = summed.astype(BF16)
    outs.append(local(input_grad_out, input_grad_ref.at[0, 0], out_sem.at[1]))
    outs[1].start()

    fw_copies = []
    for kind in range(4):
        span = gath.at[pl.ds(7 * kind, 7)]
        local(span, span, ag_recv.at[kind]).wait()
        cp = remote(span, sum_ref.at[core, pl.ds(7 * kind, 7)], fw_send.at[kind], fw_recv.at[kind], r.partner)
        cp.start()
        outs.append(local(span, sum_ref.at[core, pl.ds(7 * kind, 7)], out_sem.at[2 + kind]))
        outs[-1].start()
        fw_copies.append(cp)
    for kind in range(4):
        fw_copies[kind].wait()
    for cp in core_copies + pool_copies + [near_halo, cot_copy]:
        cp.wait_send()

    @pl.when(r.far_exists)
    def _():
        for cp in far_halos:
            cp.wait_send()

    for is_me, cp in rs_copies:
        unless(is_me, cp.wait_send)

    @pl.when(r.owner)
    def _():
        for i in range(7):
            local(ring_src, ring_src, ring_send.at[i]).wait()
        for i in range(31):
            local(final, final, ag_send.at[i]).wait()

    for cp in outs:
        cp.wait()


def hand_over(
    pooled, input_grad, total, pooled_ref, input_grad_ref, weight_ref, bias_ref, t, g, p, w, bias, get, put
):
    groups = (pl.ds(0, 9), pl.ds(9, 9), pl.ds(18, 10))
    reads = [local(total.at[:, span], t.at[:, span], get.at[i]) for i, span in enumerate(groups)]
    reads += [local(input_grad, g, get.at[3]), local(pooled, p, get.at[4])]
    for cp in reads:
        cp.start()
    writes = []
    for b in range(3):
        reads[b].wait()
        for a in range(3):
            first, at = 9 * b + 3 * a, 9 * a + 3 * b
            for h in range(2):
                w[at : at + 3, 32 * h : 32 * h + 32, :] = t[h, first : first + 3].astype(F32) * (1.0 / loss_scale)
            writes.append(local(w.at[pl.ds(at, 3)], weight_ref.at[pl.ds(at, 3)], put.at[3 * b + a]))
            writes[-1].start()
    bias[...] = t[0, taps, 0, :].astype(F32) * (1.0 / loss_scale)
    writes.append(local(bias, bias_ref, put.at[9]))
    writes[-1].start()
    reads[3].wait()
    writes.append(local(g, input_grad_ref, put.at[10]))
    writes[-1].start()
    reads[4].wait()
    writes.append(local(p, pooled_ref, put.at[11]))
    writes[-1].start()
    for cp in writes:
        cp.wait()


def block(volume, weight, conv_bias, cotangent):
    dma = pltpu.SemaphoreType.DMA
    vmem = pltpu.VMEM
    anywhere = pl.BlockSpec(memory_space=pltpu.HBM)
    shapes = (
        jax.ShapeDtypeStruct(cotangent.shape, BF16),
        jax.ShapeDtypeStruct(volume.shape, BF16),
        jax.ShapeDtypeStruct((taps, 64, 128), F32),
        jax.ShapeDtypeStruct(conv_bias.shape, F32),
    )
    sums = jax.ShapeDtypeStruct((2, blocks, 32, 128), BF16)
    results = pl.pallas_call(
        block_kernel,
        out_shape=shapes[:2] + (sums,),
        in_specs=[anywhere] * 4,
        out_specs=(anywhere,) * 3,
        scratch_shapes=[
            vmem((3, side, 2304), BF16),
            vmem((3, 3, 3, 64, 128), BF16),
            vmem((128,), F32),
            vmem((2, 8, 16, 128), BF16),
            vmem((3, 768, 256), BF16),
            vmem((3, 384, 512), BF16),
            vmem((3, cells, 768), BF16),
            vmem((3, 256, cells), BF16),
            vmem((cells, 256), F32),
            vmem((cells, 256), F32),
            vmem((cells, 256), F32),
            vmem((cells + 8, 128), F32),
            vmem((cells + 8, 128), F32),
            vmem((4, 2, 64, 128), F32),
            vmem((4, 2, 64, 128), F32),
            vmem((272, 128), F32),
            vmem((272, 128), F32),
            vmem((cells + 8, 128), F32),
            vmem((cells + 8, 128), F32),
            vmem((3, cells + 2 * side, 256), BF16),
            vmem((blocks, 64, 128), F32),
            vmem((3, cells, 128), BF16),
            vmem((3, cells, 128), BF16),
            vmem((blocks, 32, 128), BF16),
            vmem((blocks, 32, 128), BF16),
            vmem((blocks, 32, 128), BF16),
            vmem((32, per_piece, 32, 128), BF16),
            vmem((per_piece, 32, 128), BF16),
            vmem((8, per_piece, 32, 128), BF16),
            vmem((per_piece, 32, 128), BF16),
            vmem((blocks, 32, 128), BF16),
            vmem((8, 16, 128), BF16),
            vmem((side, 2048), BF16),
            dma((4,)), dma((3,)), dma((3,)), dma, dma, dma((4,)), dma((4,)), dma((2,)), dma((2,)),
            dma((9,)), dma((9,)), dma((pieces,)), dma, dma((8,)), dma, dma((32,)), dma((4,)), dma((4,)), dma((4,)), dma((6,)),
        ],
        compiler_params=pltpu.CompilerParams(
            collective_id=0, has_side_effects=True, vmem_limit_bytes=62 * 2**20
        ),
        name="conv_block",
    )(volume, weight, conv_bias, cotangent)
    pooled, input_grad, weight_grad, bias_grad = pl.pallas_call(
        hand_over,
        out_shape=shapes,
        in_specs=[anywhere] * 3,
        out_specs=(anywhere,) * 4,
        scratch_shapes=[vmem(v.shape, v.dtype) for v in (sums, shapes[1], shapes[0], shapes[2], shapes[3])]
        + [dma((5,)), dma((12,))],
        compiler_params=pltpu.CompilerParams(vmem_limit_bytes=62 * 2**20),
        name="hand_over",
    )(*results)
    return pooled, input_grad, weight_grad.reshape(weight.shape), bias_grad


def solution(mesh):
    placed = (P("sample", "space", None, None), P(), P(), P("sample", "space", None, None))
    return jax.shard_map(
        block,
        mesh=mesh,
        in_specs=placed,
        out_specs=(P("sample", "space", None, None), P("sample", "space", None, None), P(), P()),
        check_vma=False,
    )
```
